256 devices in a mesh: date: 64 (over x, z, core), row: 4 (over y).
Axes of the slice: x: 4, y: 4, z: 8, core: 2. Of those that a mesh axis runs over, the one named last changes fastest.
Arguments:
- acquisitions: bfloat16 [256, 2, 512, 2048], P('date', None, 'row'), may hold values from -4 to 4
- date_pairs: int32 [1024, 2], P('date'), may hold values from 0 to 255, as said below
- cycle_maps: int32 [1024, 128, 128], P('date', 'row'), may hold values from 0 to 1
- inverse: float32 [256, 1024], P(None, 'date'), may hold values from -0.046875 to 0.046875
Outputs:
- displacement: float32 [128, 128, 256], P('date', 'row')
The draws below stay inside these ranges and needn't reach their ends.
Inputs may be any that keep to these rules, and one draw needn't show every extreme that they name: `date_pairs`: pair k's first date lies in dates j * 4 to (j + 1) * 4 - 1 with j = k // 16; its second date is (first + gap) mod 256 with gap from 1 to 4; each aligned block of 16 pairs holds a pair with gap 4.
All inputs are finite; a program needn't handle non-finite values.
Results may differ from the reference program's by a relative error of at most 0.0003.
Values may be sent and summed in bfloat16 or wider, within the bound.
No kernel may reach another device: no remote copies, remote signals or barrier semaphores. Data moves between devices by JAX's collectives and lax.ppermute only.
A program may use at most 64 MiB of HBM per device.

```python
import math
import jax
import jax.numpy as jnp
from jax import lax

DATE_DEV = 4
COLS = 2048
LOOK_R = 4
LOOK_C = 16
PAIR_DEV = 16
DATES = 256
PAIRS = 1024
ROWS = 512
MLR = 128
MLC = 128


def draw_acquisitions(key, part):
    key = jax.random.fold_in(key, 11)
    amp_key, angle_key, screen_key = jax.random.split(key, 3)
    shape = (DATES, 1, ROWS, COLS)
    look_shape = (DATES, 1, MLR, 1, MLC, 1)
    fine_shape = (DATES, 1, MLR, LOOK_R, MLC, LOOK_C)
    screen = jax.random.uniform(screen_key, look_shape, jnp.float32, -1.05, 1.05)
    amplitude = jnp.exp(jax.random.uniform(amp_key, shape, jnp.float32, -1.2, 1.2))
    jitter = jnp.clip(0.2 * jax.random.normal(angle_key, fine_shape, jnp.float32), -0.35, 0.35)
    angle = (screen + jitter).reshape(shape)
    parts = jnp.concatenate([amplitude * jnp.cos(angle), amplitude * jnp.sin(angle)], axis=1)
    return parts.astype(jnp.bfloat16)


def draw_date_pairs(key, part):
    key = jax.random.fold_in(key, 17)
    local_key, gap_key = jax.random.split(key)
    local_date = jax.random.randint(local_key, (PAIRS,), 0, DATE_DEV)
    gap_size = jax.random.randint(gap_key, (PAIRS,), 1, DATE_DEV + 1)
    index = jnp.arange(PAIRS, dtype=jnp.int32)
    gap_size = jnp.where(index % PAIR_DEV == 0, DATE_DEV, gap_size)
    first_date = index // PAIR_DEV * DATE_DEV + local_date
    second_date = (first_date + gap_size) % DATES
    return jnp.stack([first_date, second_date], axis=1).astype(jnp.int32)


def draw_cycle_maps(key, part):
    key = jax.random.fold_in(key, 23)
    quarter = 4 * jnp.arange(MLR, dtype=jnp.int32) // MLR
    threshold = jnp.minimum(quarter, 2)
    level = jax.random.randint(key, (PAIRS, MLR, MLC), 0, 4)
    return (level <= threshold[None, :, None]).astype(jnp.int32)


def steps_of(rng, shape, cuts, smallest, largest):
    level, own = 1.0, jax.random.fold_in(rng, 6)
    for axis_at, blocks in cuts:
        steps = jnp.exp(jax.random.uniform(jax.random.fold_in(own, axis_at), (blocks,), jnp.float32, smallest / len(cuts), largest / len(cuts)))
        level = level * jnp.repeat(steps, shape[axis_at] // blocks).reshape([-1 if axis == axis_at else 1 for axis in range(len(shape))])
    return level


def scatter_about(own_key, dims, deviation, most, cuts=(), held_as=jnp.bfloat16):
    level = steps_of(own_key, dims, cuts, -0.22, 0.18) if cuts else 1.0
    drawn = jax.random.normal(own_key, dims, jnp.float32) * deviation * level
    return jnp.minimum(jnp.maximum(drawn, -most), most).astype(held_as)


def setup_inputs(seed: int = 0) -> dict:
    arg_keys = jax.random.split(jax.random.key(seed), 5)
    acquisitions = draw_acquisitions(jax.random.fold_in(arg_keys[4], 71), 0)
    date_pairs = draw_date_pairs(jax.random.fold_in(arg_keys[4], 71), 0)
    cycle_maps = draw_cycle_maps(jax.random.fold_in(arg_keys[4], 71), 0)
    inverse = scatter_about(arg_keys[3], (DATES, PAIRS), (16 * PAIRS) ** -0.5, 0.046875, ((1, 64),), jnp.float32)
    return {"acquisitions": acquisitions, "date_pairs": date_pairs, "cycle_maps": cycle_maps, "inverse": inverse}


TWO_PI = 2.0 * math.pi


def form_pair(images, pair_dates):
    reference_image = lax.dynamic_index_in_dim(images, pair_dates[0], 0, keepdims=False).astype(jnp.float32)
    second_image = lax.dynamic_index_in_dim(images, pair_dates[1], 0, keepdims=False).astype(jnp.float32)
    real_part = reference_image[0] * second_image[0] + reference_image[1] * second_image[1]
    imag_part = reference_image[1] * second_image[0] - reference_image[0] * second_image[1]
    height, width = real_part.shape
    real_look = real_part.reshape(height // LOOK_R, LOOK_R, width // LOOK_C, LOOK_C).sum(axis=(1, 3))
    imag_look = imag_part.reshape(height // LOOK_R, LOOK_R, width // LOOK_C, LOOK_C).sum(axis=(1, 3))
    return jnp.arctan2(imag_look, real_look)


def reference(acquisitions, date_pairs, cycle_maps, inverse):
    def single(pair_dates):
        return form_pair(acquisitions, pair_dates)

    wrapped = lax.map(single, date_pairs)
    phase = wrapped - TWO_PI * cycle_maps.astype(jnp.float32)
    band_mean = jnp.sum(phase, axis=(1, 2), keepdims=True) / (MLR * MLC)
    centered = phase - band_mean
    pixel_rows = centered.reshape(PAIRS, MLR * MLC)
    result = jnp.dot(inverse, pixel_rows, precision=lax.Precision.HIGHEST, preferred_element_type=jnp.float32)
    return result.reshape(DATES, MLR, MLC).transpose(2, 1, 0)
```

```python
from functools import partial
import math

import jax
import jax.numpy as jnp
from jax import lax
from jax.experimental import pallas as pl
from jax.experimental.pallas import tpu as pltpu
from jax.sharding import PartitionSpec as P

LOOK_R = 4
LOOK_C = 16
TWO_PI = 2.0 * math.pi
CHUNKS = 4
STEP = 256
LANES = 128


def passed_along(value, axis, steps):
    count = lax.axis_size(axis)
    pairs = [(source, (source + steps) % count) for source in range(count)]
    return lax.ppermute(value, axis, pairs)


def phase_kernel(pairs_ref, top_own, top_next, low_prev, low_own, cycles, sums_in, *rest):
    payload, sums, images, high, low = rest[-5:]
    group, _, rows, width = top_own.shape
    looks = rows // LOOK_R
    pair_count = pairs_ref.shape[0] // 4
    out_cols = width // LOOK_C

    @pl.when(pl.program_id(0) == 0)
    def _():
        sums[...] = sums_in[...]

    for half, (first, second) in enumerate(((top_own, top_next), (low_prev, low_own))):
        for at, source in enumerate((first, second)):
            for date in range(group):
                for part in range(2):
                    for tile in range(width // LANES):
                        images[half, at * group + date, part, tile] = source[
                            date, part, :, tile * LANES : (tile + 1) * LANES
                        ].astype(jnp.float32)

    for half in range(2):

        @pl.loop(0, pair_count)
        def _(pair, half=half):
            a = pairs_ref[(half * pair_count + pair) * 2]
            b = pairs_ref[(half * pair_count + pair) * 2 + 1]
            for tile in range(width // LANES):
                real = imag = None
                for step in range(LOOK_R):
                    at = pl.ds(step, looks, stride=LOOK_R)
                    a0, a1 = images[half, a, 0, tile, at, :], images[half, a, 1, tile, at, :]
                    b0, b1 = images[half, b, 0, tile, at, :], images[half, b, 1, tile, at, :]
                    re, im = a0 * b0 + a1 * b1, a1 * b0 - a0 * b1
                    real, imag = (re, im) if real is None else (real + re, imag + im)
                for part, value in enumerate((real, imag)):
                    base = part * pair_count * 2 * looks + half * looks
                    place = pl.ds(pl.multiple_of(pair * 2 * looks + base, 16), looks)
                    head = value.astype(jnp.bfloat16)
                    high[place, tile * LANES : (tile + 1) * LANES] = head
                    low[place, tile * LANES : (tile + 1) * LANES] = (value - head.astype(jnp.float32)).astype(
                        jnp.bfloat16
                    )

    shape = (out_cols, width)
    picked = lax.broadcasted_iota(jnp.int32, shape, 1) // LOOK_C == lax.broadcasted_iota(jnp.int32, shape, 0)
    picked = jnp.where(picked, 1.0, 0.0).astype(jnp.bfloat16)
    turned = (((1,), (1,)), ((), ()))
    looked = lax.dot_general(picked, high[...], turned, preferred_element_type=jnp.float32)
    looked += lax.dot_general(picked, low[...], turned, preferred_element_type=jnp.float32)
    half_width = looked.shape[1] // 2
    real, imag = looked[:, :half_width], looked[:, half_width:]
    phase = jnp.arctan2(imag, real) - cycles[...]
    total = jnp.sum(phase, axis=0, keepdims=True)
    blocks = half_width // LANES
    for q in range(blocks):
        payload[pl.ds(q, out_cols, stride=blocks), :] = phase[:, q * LANES : (q + 1) * LANES]
        sums[q : q + 1, :] += total[:, q * LANES : (q + 1) * LANES]


def phases(chunk, chunk_width, pairs, acquisitions, following, previous, cycles, sums, payload):
    group, _, height, width = acquisitions.shape
    rows = height // 2
    steps = chunk_width // STEP
    lanes = cycles.shape[1]
    out_cols = STEP // LOOK_C
    block_rows = out_cols * lanes // LANES
    payload_shape = (cycles.shape[0] * lanes // LANES, LANES)
    looks = rows // LOOK_R
    pair_count = lanes // (2 * looks)
    whole = (group, 2, rows, STEP)

    in_specs = [
        pl.BlockSpec(whole, lambda i, p: (0, 0, 0, chunk * steps + i)),
        pl.BlockSpec(whole, lambda i, p: (0, 0, 0, i)),
        pl.BlockSpec(whole, lambda i, p: (0, 0, 0, i)),
        pl.BlockSpec(whole, lambda i, p: (0, 0, 1, chunk * steps + i)),
        pl.BlockSpec((out_cols, lanes), lambda i, p: (chunk * steps + i, 0)),
        pl.BlockSpec((8, LANES), lambda i, p: (0, 0)),
    ]
    operands = [pairs, acquisitions, following, previous, acquisitions, cycles, sums]
    aliases = {}
    if payload is not None:
        in_specs.append(pl.BlockSpec(memory_space=pl.ANY))
        aliases = {len(operands): 0}
        operands.append(payload)
    return pl.pallas_call(
        phase_kernel,
        grid_spec=pltpu.PrefetchScalarGridSpec(
            num_scalar_prefetch=1,
            grid=(steps,),
            in_specs=in_specs,
            out_specs=[
                pl.BlockSpec((block_rows, LANES), lambda i, p: (chunk * steps + i, 0)),
                pl.BlockSpec((8, LANES), lambda i, p: (0, 0)),
            ],
            scratch_shapes=[
                pltpu.VMEM((2, 2 * group, 2, STEP // LANES, rows, LANES), jnp.float32),
                pltpu.VMEM((2 * lanes, STEP), jnp.bfloat16),
                pltpu.VMEM((2 * lanes, STEP), jnp.bfloat16),
            ],
        ),
        out_shape=[
            jax.ShapeDtypeStruct(payload_shape, jnp.float32),
            jax.ShapeDtypeStruct((8, LANES), jnp.float32),
        ],
        input_output_aliases=aliases,
        compiler_params=pltpu.CompilerParams(vmem_limit_bytes=24 << 20),
        cost_estimate=pl.CostEstimate(
            flops=10 * pair_count * height * chunk_width,
            bytes_accessed=group * 2 * height * chunk_width * 4,
            transcendentals=0,
        ),
        name="phases",
    )(*operands)


def invert_kernel(band_pixels, received, inverse, sums, out, left):
    sources = inverse.shape[0] // 16
    pair_count = 16
    blocks = 4
    per = pair_count // blocks
    rows = LANES // per
    pixels = out.shape[0]

    def aligned(value):
        rolled = pltpu.roll(value, sources - 1, 0)
        lane = lax.broadcasted_iota(jnp.int32, value.shape, 1) % rows
        return jnp.where(lane < rows // 2, value, rolled).T

    left[pixels:, :] = jnp.zeros((left.shape[0] - pixels, left.shape[1]), jnp.float32)
    for q in range(blocks):
        for col in range(pixels // rows):
            turned = aligned(received[pl.ds(col * blocks + q, sources, stride=8), :])
            for at in range(per):
                pair = q * per + at
                left[col * rows : (col + 1) * rows, pair * sources : (pair + 1) * sources] = turned[
                    at * rows : (at + 1) * rows
                ]
        turned = aligned(sums[pl.ds(q, sources, stride=8), :])
        for at in range(per):
            pair = q * per + at
            left[pixels : pixels + 1, pair * sources : (pair + 1) * sources] = jnp.sum(
                turned[at * rows : (at + 1) * rows], axis=0, keepdims=True
            )
    product = jnp.dot(
        left[...], inverse[...], precision=lax.Precision.HIGHEST, preferred_element_type=jnp.float32
    )
    out[...] = product[:pixels] - product[pixels : pixels + 1] * (1.0 / band_pixels)


def invert(received, inverse, sums, pixels, band_pixels):
    total_pairs, dates = inverse.shape
    return pl.pallas_call(
        partial(invert_kernel, band_pixels),
        in_specs=[pl.BlockSpec(memory_space=pltpu.VMEM)] * 3,
        out_specs=pl.BlockSpec(memory_space=pltpu.VMEM),
        out_shape=jax.ShapeDtypeStruct((pixels, dates), jnp.float32),
        scratch_shapes=[
            pltpu.VMEM((pixels + 8, total_pairs), jnp.float32),
        ],
        compiler_params=pltpu.CompilerParams(vmem_limit_bytes=24 << 20),
        name="invert",
    )(received, inverse, sums)


def body(acquisitions, date_pairs, cycle_maps, inverse):
    group, _, height, width = acquisitions.shape
    devices = lax.axis_size("date")
    total_dates = group * devices
    pair_count, look_rows, look_cols = cycle_maps.shape
    rows = height // 2
    half = look_rows // 2

    base = lax.axis_index("date") * group
    local = jnp.stack([date_pairs[:, 0] - base, (date_pairs[:, 1] - base + total_dates) % total_dates], axis=1)
    pairs = jnp.concatenate([local, passed_along(local, "date", 1)], axis=0).reshape(-1)

    low_cycles = passed_along(cycle_maps[:, half:].astype(jnp.bfloat16), "date", 1)
    cycles = jnp.concatenate(
        [cycle_maps[:, :half].astype(jnp.float32), low_cycles.astype(jnp.float32)], axis=1
    )
    cycles = (TWO_PI * cycles).reshape(pair_count * look_rows, look_cols).T

    whole_inverse = lax.all_gather(inverse.T, "date", axis=1).reshape(-1, total_dates)

    chunk_width = width // CHUNKS
    following, previous = [], []
    for chunk in range(CHUNKS):
        cols = slice(chunk * chunk_width, (chunk + 1) * chunk_width)
        following.append(passed_along(acquisitions[:, :, :rows, cols], "date", -1))
        previous.append(passed_along(acquisitions[:, :, rows:, cols], "date", 1))

    payload, sums = None, jnp.zeros((8, LANES), jnp.float32)
    for chunk in range(CHUNKS):
        payload, sums = phases(
            chunk, chunk_width, pairs, acquisitions, following[chunk], previous[chunk], cycles, sums, payload
        )

    received = lax.all_to_all(
        payload.reshape(devices, -1, LANES), "date", split_axis=0, concat_axis=0, tiled=True
    ).reshape(payload.shape)
    sums = lax.psum(sums, "row")
    sums = lax.all_gather(sums, "date", axis=0, tiled=True)
    out_cols = look_cols // devices
    band_pixels = look_rows * look_cols * lax.axis_size("row")
    result = invert(received, whole_inverse, sums, out_cols * look_rows, band_pixels)
    return result.reshape(out_cols, look_rows, total_dates)


def solution(mesh):
    return jax.shard_map(
        body,
        mesh=mesh,
        in_specs=(
            P("date", None, "row", None),
            P("date", None),
            P("date", "row", None),
            P(None, "date"),
        ),
        out_specs=P("date", "row", None),
        check_vma=False,
    )
```

```python
from functools import partial
import math

import jax
import jax.numpy as jnp
from jax import lax
from jax.experimental import pallas as pl
from jax.experimental.pallas import tpu as pltpu
from jax.sharding import PartitionSpec as P

LOOK_R = 4
LOOK_C = 16
TWO_PI = 2.0 * math.pi
CODES = 32767.0 / TWO_PI
CUTS = (0, 1280, 2048)
STEP = 256
LANES = 128
SUM_ROWS = (2, 3, 6, 7)


def passed_along(value, axis, steps):
    count = lax.axis_size(axis)
    pairs = [(source, (source + steps) % count) for source in range(count)]
    return lax.ppermute(value, axis, pairs)


def phase_kernel(first_step, steps, combos_ref, top_own, top_next, low_prev, low_own, cycles, *rest):
    payload, sums, images, products, high, low = rest[-6:]
    group, _, rows, width = top_own.shape
    looks = rows // LOOK_R
    pair_count = combos_ref.shape[0] // 2
    out_cols = width // LOOK_C
    tiles = width // LANES
    sets = looks // 8
    step_at = pl.program_id(0)

    @pl.when(step_at == 0)
    def _():
        if first_step:
            earlier, earlier_sums = rest[0], rest[1]
            done = first_step * out_cols * 4
            payload[:done, :] = earlier[:done, :]
            sums[...] = earlier_sums[...]
        else:
            sums[...] = jnp.zeros_like(sums)

    for half, (first, second) in enumerate(((top_own, top_next), (low_prev, low_own))):
        for at, source in enumerate((first, second)):
            for date in range(group):
                for part in range(2):
                    for tile in range(tiles):
                        images[half, at * group + date, part, tile] = source[
                            date, part, :, tile * LANES : (tile + 1) * LANES
                        ].astype(jnp.float32)

    @pl.loop(0, 2 * tiles * sets)
    def _(index):
        half, tile, block = index // (tiles * sets), index // sets % tiles, index % sets
        real, imag = [None] * (group * group), [None] * (group * group)
        for step in range(LOOK_R):
            at = pl.ds(block * 8 * LOOK_R + step, 8, stride=LOOK_R)
            parts = [[images[half, date, part, tile, at, :] for part in range(2)] for date in range(2 * group)]
            for date in range(group):
                a0, a1 = parts[date]
                for gap in range(group):
                    b0, b1 = parts[date + gap + 1]
                    combo = date * group + gap
                    re, im = a0 * b0 + a1 * b1, a1 * b0 - a0 * b1
                    real[combo] = re if step == 0 else real[combo] + re
                    imag[combo] = im if step == 0 else imag[combo] + im
        place = pl.ds(pl.multiple_of(block * 8, 8), 8)
        for combo in range(group * group):
            products[half, combo, 0, tile, place, :] = real[combo]
            products[half, combo, 1, tile, place, :] = imag[combo]

    for half in range(2):

        @pl.loop(0, pair_count)
        def _(pair, half=half):
            combo = combos_ref[half * pair_count + pair]
            for part in range(2):
                base = part * pair_count * 2 * looks + half * looks
                place = pl.ds(pl.multiple_of(pair * 2 * looks + base, 16), looks)
                for tile in range(tiles):
                    value = products[half, combo, part, tile]
                    head = value.astype(jnp.bfloat16)
                    high[place, tile * LANES : (tile + 1) * LANES] = head
                    low[place, tile * LANES : (tile + 1) * LANES] = (value - head.astype(jnp.float32)).astype(
                        jnp.bfloat16
                    )

    shape = (out_cols, width)
    picked = lax.broadcasted_iota(jnp.int32, shape, 1) // LOOK_C == lax.broadcasted_iota(jnp.int32, shape, 0)
    picked = jnp.where(picked, 1.0, 0.0).astype(jnp.bfloat16)
    turned = (((1,), (1,)), ((), ()))
    looked = lax.dot_general(picked, high[...], turned, preferred_element_type=jnp.float32)
    looked += lax.dot_general(picked, low[...], turned, preferred_element_type=jnp.float32)
    half_width = looked.shape[1] // 2
    real, imag = looked[:, :half_width], looked[:, half_width:]
    imag = jnp.where(imag == 0.0, 0.0, imag)
    phase = jnp.arctan2(imag, real) - cycles[...]
    codes = jnp.round((phase + math.pi) * CODES)
    blocks = half_width // LANES
    total = jnp.sum(codes, axis=0, keepdims=True).astype(jnp.int32)
    codes = codes.astype(jnp.int32)
    for q in range(blocks):
        sums[q : q + 1, :] += total[:, q * LANES : (q + 1) * LANES]
    base = (step_at + first_step) * (out_cols * 4)
    for word in range(blocks // 2):
        left = codes[:, 2 * word * LANES : (2 * word + 1) * LANES]
        right = codes[:, (2 * word + 1) * LANES : (2 * word + 2) * LANES]
        payload[pl.ds(base + word, out_cols, stride=4), :] = (left << 16) | (right & 0xFFFF)

    if (first_step + steps) * out_cols * 4 == payload.shape[0]:

        @pl.when(step_at == steps - 1)
        def _():
            for q in range(blocks):
                count = payload.shape[0] // 8
                payload[pl.ds(SUM_ROWS[q], count, stride=8), :] = jnp.broadcast_to(
                    sums[q : q + 1, :], (count, LANES)
                )


def phases(start, stop, combos, acquisitions, following, previous, cycles, earlier):
    group, _, height, width = acquisitions.shape
    rows = height // 2
    first_step, steps = start // STEP, (stop - start) // STEP
    lanes = cycles.shape[1]
    out_cols = STEP // LOOK_C
    payload_shape = (cycles.shape[0] * lanes // LANES, LANES)
    looks = rows // LOOK_R
    tiles = STEP // LANES
    whole = (group, 2, rows, STEP)

    in_specs = [
        pl.BlockSpec(whole, lambda i, p: (0, 0, 0, first_step + i)),
        pl.BlockSpec(whole, lambda i, p: (0, 0, 0, i)),
        pl.BlockSpec(whole, lambda i, p: (0, 0, 0, i)),
        pl.BlockSpec(whole, lambda i, p: (0, 0, 1, first_step + i)),
        pl.BlockSpec((out_cols, lanes), lambda i, p: (first_step + i, 0)),
    ]
    outs = [
        pl.BlockSpec(payload_shape, lambda i, p: (0, 0)),
        pl.BlockSpec((8, LANES), lambda i, p: (0, 0)),
    ]
    operands = [combos, acquisitions, following, previous, acquisitions, cycles, *earlier]
    return pl.pallas_call(
        partial(phase_kernel, first_step, steps),
        grid_spec=pltpu.PrefetchScalarGridSpec(
            num_scalar_prefetch=1,
            grid=(steps,),
            in_specs=in_specs + outs[: len(earlier)],
            out_specs=outs,
            scratch_shapes=[
                pltpu.VMEM((2, 2 * group, 2, tiles, rows, LANES), jnp.float32),
                pltpu.VMEM((2, group * group, 2, tiles, looks, LANES), jnp.float32),
                pltpu.VMEM((2 * lanes, STEP), jnp.bfloat16),
                pltpu.VMEM((2 * lanes, STEP), jnp.bfloat16),
            ],
        ),
        out_shape=[
            jax.ShapeDtypeStruct(payload_shape, jnp.int32),
            jax.ShapeDtypeStruct((8, LANES), jnp.int32),
        ],
        compiler_params=pltpu.CompilerParams(vmem_limit_bytes=24 << 20),
        cost_estimate=pl.CostEstimate(
            flops=8 * group * group * height * (stop - start),
            bytes_accessed=group * 2 * height * (stop - start) * 4,
            transcendentals=0,
        ),
        name="phases",
    )(*operands)


def placed_kernel(row_ref, *refs):
    *pieces, out = refs
    per, sources, _ = pieces[0].shape
    for offset, piece in enumerate(pieces):
        owner = lax.rem(row_ref[0] - offset + len(pieces), len(pieces))
        for at in range(per):
            start = pl.multiple_of((owner * per + at) * sources, 8)
            out[pl.ds(start, sources), :] = piece[at]


def whole_inverse(inverse):
    devices, row_count = lax.axis_size("date"), lax.axis_size("row")
    dates, pair_count = inverse.shape
    per = pair_count // row_count
    mine = lax.dynamic_slice_in_dim(inverse.T, lax.axis_index("row") * per, per, axis=0)
    sent = jnp.broadcast_to(mine.reshape(1, 2, per * dates // 2), (devices // 2, 2, per * dates // 2))
    sent = sent.reshape(devices, per * dates // (2 * LANES), LANES)
    got = lax.all_to_all(sent, "date", split_axis=0, concat_axis=0, tiled=True)
    got = got.reshape(devices, per // 2, dates).transpose(1, 0, 2)
    other = lax.ppermute(got, "date", [(at, at ^ 1) for at in range(devices)])
    odd = lax.axis_index("date") % 2
    got = jnp.concatenate([jnp.where(odd == 0, got, other), jnp.where(odd == 0, other, got)], axis=0)
    pieces = [got] + [passed_along(got, "row", step) for step in range(1, row_count)]
    return pl.pallas_call(
        placed_kernel,
        in_specs=[pl.BlockSpec(memory_space=pltpu.SMEM)] + [pl.BlockSpec(memory_space=pltpu.VMEM)] * row_count,
        out_specs=pl.BlockSpec(memory_space=pltpu.VMEM),
        out_shape=jax.ShapeDtypeStruct((pair_count * devices, dates), jnp.float32),
        name="placed",
    )(lax.axis_index("row").reshape(1), *pieces)


def invert_kernel(band_pixels, received, inverse, out, bias, left):
    pair_count, blocks = 16, 4
    sources = inverse.shape[0] // pair_count
    per = pair_count // blocks
    rows = LANES // per
    pixels = out.shape[0]

    def aligned(words):
        value = words.astype(jnp.float32)
        rolled = pltpu.roll(value, sources - 1, 0)
        lane = lax.broadcasted_iota(jnp.int32, value.shape, 1) % rows
        return jnp.where(lane < rows // 2, value, rolled).T

    left[pixels:, :] = jnp.zeros((left.shape[0] - pixels, left.shape[1]), jnp.float32)
    for col in range(pixels // rows):
        for word in range(blocks // 2):
            words = received[pl.ds(col * 4 + word, sources, stride=8), :]
            for side, value in enumerate((words >> 16, (words << 16) >> 16)):
                turned = aligned(value)
                for at in range(per):
                    pair = (2 * word + side) * per + at
                    left[col * rows : (col + 1) * rows, pair * sources : (pair + 1) * sources] = turned[
                        at * rows : (at + 1) * rows
                    ]
    for q in range(blocks):
        turned = aligned(received[pl.ds(SUM_ROWS[q], sources, stride=8), :])
        for at in range(per):
            pair = q * per + at
            left[pixels : pixels + 1, pair * sources : (pair + 1) * sources] = jnp.sum(
                turned[at * rows : (at + 1) * rows], axis=0, keepdims=True
            )
    product = jnp.dot(
        left[...], inverse[...], precision=lax.Precision.HIGHEST, preferred_element_type=jnp.float32
    )
    out[...] = product[:pixels] * (1.0 / CODES)
    bias[...] = product[pixels:] * (1.0 / (CODES * band_pixels))


def invert(received, inverse, pixels, band_pixels):
    total_pairs, dates = inverse.shape
    return pl.pallas_call(
        partial(invert_kernel, band_pixels),
        in_specs=[pl.BlockSpec(memory_space=pltpu.VMEM)] * 2,
        out_specs=[pl.BlockSpec(memory_space=pltpu.VMEM)] * 2,
        out_shape=[
            jax.ShapeDtypeStruct((pixels, dates), jnp.float32),
            jax.ShapeDtypeStruct((8, dates), jnp.float32),
        ],
        scratch_shapes=[pltpu.VMEM((pixels + 8, total_pairs), jnp.float32)],
        compiler_params=pltpu.CompilerParams(vmem_limit_bytes=24 << 20),
        name="invert",
    )(received, inverse)


def body(acquisitions, date_pairs, cycle_maps, inverse):
    group, _, height, width = acquisitions.shape
    devices = lax.axis_size("date")
    total_dates = group * devices
    pair_count, look_rows, look_cols = cycle_maps.shape
    rows = height // 2
    half = look_rows // 2

    sliced = [
        (acquisitions[:, :, :rows, start:stop], acquisitions[:, :, rows:, start:stop])
        for start, stop in zip(CUTS[:-1], CUTS[1:])
    ]
    sliced, date_pairs, cycle_maps, inverse = lax.optimization_barrier((sliced, date_pairs, cycle_maps, inverse))
    following = [passed_along(upper, "date", -1) for upper, _ in sliced]
    previous = [passed_along(lower, "date", 1) for _, lower in sliced]

    base = lax.axis_index("date") * group
    gaps = (date_pairs[:, 1] - date_pairs[:, 0] + total_dates) % total_dates
    combos = (date_pairs[:, 0] - base) * group + gaps - 1
    named = jnp.broadcast_to(combos[:, None, None], (pair_count, half, look_cols))
    low_data = jnp.stack([cycle_maps[:, half:], named]).astype(jnp.bfloat16)
    low_data = passed_along(low_data, "date", 1)
    combos = jnp.concatenate([combos, low_data[1, :, 0, 0].astype(jnp.int32)])
    cycles = jnp.concatenate([cycle_maps[:, :half].astype(jnp.float32), low_data[0].astype(jnp.float32)], axis=1)
    cycles = (TWO_PI * cycles).reshape(pair_count * look_rows, look_cols).T

    inverse = whole_inverse(inverse)

    earlier = ()
    for chunk, (start, stop) in enumerate(zip(CUTS[:-1], CUTS[1:])):
        earlier = phases(
            start, stop, combos, acquisitions, following[chunk], previous[chunk], cycles, earlier
        )

    payload = earlier[0]
    received = lax.all_to_all(
        payload.reshape(devices, -1, LANES), "date", split_axis=0, concat_axis=0, tiled=True
    ).reshape(payload.shape)
    out_cols = look_cols // devices
    row_count = lax.axis_size("row")
    result, bias = invert(received, inverse, out_cols * look_rows, look_rows * look_cols * row_count)
    for step in range(1, row_count):
        result = result - passed_along(bias, "row", step)[:1]
    result = result - bias[:1]
    return result.reshape(out_cols, look_rows, total_dates)


def solution(mesh):
    return jax.shard_map(
        body,
        mesh=mesh,
        in_specs=(
            P("date", None, "row", None),
            P("date", None),
            P("date", "row", None),
            P(None, "date"),
        ),
        out_specs=P("date", "row", None),
        check_vma=False,
    )
```

```python
from functools import partial
import math

import jax
import jax.numpy as jnp
from jax import lax
from jax.experimental import pallas as pl
from jax.experimental.pallas import tpu as pltpu
from jax.sharding import PartitionSpec as P

LOOK_R = 4
LOOK_C = 16
TWO_PI = 2.0 * math.pi
CODES = 32767.0 / TWO_PI
INNER = ((0, 1024), (1024, 2048))
OUTER = ((0, 1024), (1024, 2048))
ORDER = ((0, 0), (0, 1), (1, 0), (1, 1))
STEP = 512
MESSAGE = 5
LANES = 128


def passed_along(value, axis, steps):
    count = lax.axis_size(axis)
    pairs = [(source, (source + steps) % count) for source in range(count)]
    return lax.ppermute(value, axis, pairs)


def phase_kernel(slot, first_step, steps, final, scalars, own, other, cycles, *rest):
    payload, sums, images, products, high, low, words = rest[-7:]
    rest = rest[:-7]
    group, _, rows, width = own.shape
    looks = rows // LOOK_R
    pair_count = group * group
    out_cols = width // LOOK_C
    tiles = width // LANES
    sets = looks // 8
    half, own_at = scalars[0], scalars[2]
    step_at = pl.program_id(0)

    @pl.when(step_at == 0)
    def _():
        if len(rest) > 1:
            payload[...] = rest[1][...]
            sums[...] = rest[2][...]
        else:
            sums[...] = jnp.zeros_like(sums)

    @pl.loop(0, 2 * group)
    def _(index):
        date, part = index // 2, index % 2
        for source, start in ((own, own_at), (other, group - own_at)):
            for tile in range(tiles):
                images[start + date, part, tile] = source[
                    date, part, :, tile * LANES : (tile + 1) * LANES
                ].astype(jnp.float32)

    @pl.loop(0, tiles * sets)
    def _(index):
        tile, block = index // sets, index % sets
        real, imag = [None] * pair_count, [None] * pair_count
        for step in range(LOOK_R):
            at = pl.ds(block * 8 * LOOK_R + step, 8, stride=LOOK_R)
            parts = [[images[date, part, tile, at, :] for part in range(2)] for date in range(2 * group)]
            for date in range(group):
                a0, a1 = parts[date]
                for gap in range(group):
                    b0, b1 = parts[date + gap + 1]
                    combo = date * group + gap
                    re, im = a0 * b0 + a1 * b1, a1 * b0 - a0 * b1
                    real[combo] = re if step == 0 else real[combo] + re
                    imag[combo] = im if step == 0 else imag[combo] + im
        place = pl.ds(pl.multiple_of(block * 8, 8), 8)
        for combo in range(pair_count):
            products[combo, 0, tile, place, :] = real[combo]
            products[combo, 1, tile, place, :] = imag[combo]

    @pl.loop(0, pair_count)
    def _(pair):
        combo = scalars[4 + pair]
        for part in range(2):
            place = pl.ds(pl.multiple_of((part * pair_count + pair) * looks, 16), looks)
            for tile in range(tiles):
                value = products[combo, part, tile]
                head = value.astype(jnp.bfloat16)
                high[place, tile * LANES : (tile + 1) * LANES] = head
                low[place, tile * LANES : (tile + 1) * LANES] = (value - head.astype(jnp.float32)).astype(
                    jnp.bfloat16
                )

    shape = (out_cols, width)
    picked = lax.broadcasted_iota(jnp.int32, shape, 1) // LOOK_C == lax.broadcasted_iota(jnp.int32, shape, 0)
    picked = jnp.where(picked, 1.0, 0.0).astype(jnp.bfloat16)
    turned = (((1,), (1,)), ((), ()))
    looked = lax.dot_general(picked, high[...], turned, preferred_element_type=jnp.float32)
    looked += lax.dot_general(picked, low[...], turned, preferred_element_type=jnp.float32)
    half_width = looked.shape[1] // 2
    real, imag = looked[:, :half_width], looked[:, half_width:]
    imag = jnp.where(imag == 0.0, 0.0, imag)
    phase = jnp.arctan2(imag, real) - cycles[...]
    codes = jnp.round((phase + math.pi) * CODES)
    total = jnp.sum(codes, axis=0, keepdims=True).astype(jnp.int32)
    codes = codes.astype(jnp.int32)
    for octet in range(2):
        row = 2 * slot + octet
        sums[row : row + 1, :] += total[:, octet * LANES : (octet + 1) * LANES]
    words[...] = (codes[:, :LANES] << 16) | (codes[:, LANES:] & 0xFFFF)
    base = (step_at + first_step) * (out_cols // 2) * MESSAGE
    for col in range(2):
        place = pl.ds(base + 2 * col + half, out_cols // 2, stride=MESSAGE)
        payload[place, :] = words[pl.ds(col, out_cols // 2, stride=2), :]

    if final:

        @pl.when(step_at == steps - 1)
        def _():
            total = sums[...]
            for step in (8, 4, 2, 1):
                total += pltpu.roll(total, LANES - step, 1)
            lane = lax.broadcasted_iota(jnp.int32, (1, LANES), 1) % looks
            line = rest[0][0:1, :]
            for at in range(2):
                of = half if at == slot else 1 - half
                for octet in range(2):
                    row = 2 * at + octet
                    for side in range(2):
                        lanes_at = 2 * side + octet
                        moved = pltpu.roll(total, lanes_at, 1)[row : row + 1]
                        line = jnp.where((lane == lanes_at) & (of == side), moved, line)
            count = payload.shape[0] // MESSAGE
            payload[pl.ds(4, count, stride=MESSAGE), :] = jnp.broadcast_to(line, (count, LANES))


def phases(slot, start, stop, final, scalars, acquisitions, other, cycles, line, earlier):
    group, _, height, width = acquisitions.shape
    rows = height // 2
    first_step, steps = start // STEP, (stop - start) // STEP
    lanes = cycles.shape[1] // 2
    out_cols = STEP // LOOK_C
    payload_shape = (cycles.shape[0] // 2 * MESSAGE, LANES)
    looks = rows // LOOK_R
    tiles = STEP // LANES

    in_specs = [
        pl.BlockSpec((group, 2, rows, STEP), lambda i, p: (0, 0, p[1], first_step + i)),
        pl.BlockSpec((None, group, 2, rows, STEP), lambda i, p: (p[3], 0, 0, 0, i)),
        pl.BlockSpec((out_cols, lanes), lambda i, p: (first_step + i, p[0])),
        pl.BlockSpec((8, LANES), lambda i, p: (0, 0)),
    ]
    outs = [
        pl.BlockSpec(payload_shape, lambda i, p: (0, 0)),
        pl.BlockSpec((8, LANES), lambda i, p: (0, 0)),
    ]
    return pl.pallas_call(
        partial(phase_kernel, slot, first_step, steps, final),
        grid_spec=pltpu.PrefetchScalarGridSpec(
            num_scalar_prefetch=1,
            grid=(steps,),
            in_specs=in_specs + outs[: len(earlier)],
            out_specs=outs,
            scratch_shapes=[
                pltpu.VMEM((2 * group, 2, tiles, rows, LANES), jnp.float32),
                pltpu.VMEM((group * group, 2, tiles, looks, LANES), jnp.float32),
                pltpu.VMEM((2 * lanes, STEP), jnp.bfloat16),
                pltpu.VMEM((2 * lanes, STEP), jnp.bfloat16),
                pltpu.VMEM((out_cols, LANES), jnp.int32),
            ],
        ),
        out_shape=[
            jax.ShapeDtypeStruct(payload_shape, jnp.int32),
            jax.ShapeDtypeStruct((8, LANES), jnp.int32),
        ],
        compiler_params=pltpu.CompilerParams(vmem_limit_bytes=60 << 20),
        cost_estimate=pl.CostEstimate(
            flops=8 * group * group * rows * (stop - start),
            bytes_accessed=group * 4 * rows * (stop - start) * 2,
            transcendentals=0,
        ),
        name="phases",
    )(scalars, acquisitions, other, cycles, line, *earlier)


def coded_inverse(inverse):
    turned = inverse.T
    peak = jnp.max(jnp.abs(turned), axis=1, keepdims=True)
    exponent = jnp.clip(jnp.floor(jnp.log2(peak)) + 1.0, -100.0, 100.0)
    codes = jnp.round(turned * jnp.exp2(-exponent) * 32767.0).astype(jnp.int32)
    words = (codes[:, :LANES] << 16) | (codes[:, LANES:] & 0xFFFF)
    return words, exponent[:, 0].astype(jnp.int32)


def exponent_line(exponent):
    spread = exponent.reshape(2, -1).T
    spread = jnp.pad(spread, ((0, 0), (4, LANES // spread.shape[0] - 6)))
    return jnp.broadcast_to(spread.reshape(1, LANES), (8, LANES))


def sent_inverse(words):
    devices, row_count = lax.axis_size("date"), lax.axis_size("row")
    per = words.shape[0] // row_count
    mine = lax.dynamic_slice_in_dim(words, lax.axis_index("row") * per, per, axis=0)
    sent = jnp.broadcast_to(mine[None], (devices, per, LANES))
    got = lax.all_to_all(sent, "date", split_axis=0, concat_axis=0, tiled=True)
    return got.transpose(1, 0, 2)


def invert_kernel(band_pixels, received, inverse, out, bias, left, right):
    pair_count = 16
    sources = inverse.shape[0] // pair_count
    looks = LANES * 2 // pair_count
    pixels = out.shape[0]

    def aligned(words, half):
        value = words.astype(jnp.float32)
        return (pltpu.roll(value, sources - 1, 0) if half else value).T

    right[:, :LANES] = (inverse[...] >> 16).astype(jnp.float32)
    right[:, LANES:] = ((inverse[...] << 16) >> 16).astype(jnp.float32)
    line = received[pl.ds(4, sources, stride=MESSAGE), :]
    lines = aligned(line, 0), aligned(line, 1)
    scales = []
    for pair in range(pair_count):
        octet, at = pair // 8, pair % 8 * looks
        scales.append(jnp.exp2(lines[0][at + 4 + octet : at + 5 + octet]) * (1.0 / 32767.0))
        total = lines[0][at + octet : at + octet + 1] + lines[1][at + 2 + octet : at + 3 + octet]
        left[pixels:, pair * sources : (pair + 1) * sources] = jnp.broadcast_to(
            total * scales[pair], (left.shape[0] - pixels, sources)
        )
    for half in range(2):
        for col in range(pixels // (2 * looks)):
            words = received[pl.ds(col * 2 + half, sources, stride=MESSAGE), :]
            for octet, value in enumerate((words >> 16, (words << 16) >> 16)):
                turned = aligned(value, half)
                for at in range(8):
                    pair = octet * 8 + at
                    row = (col * 2 + half) * looks
                    left[row : row + looks, pair * sources : (pair + 1) * sources] = (
                        turned[at * looks : (at + 1) * looks] * scales[pair]
                    )
    product = jnp.dot(
        left[...], right[...], precision=lax.Precision.HIGHEST, preferred_element_type=jnp.float32
    )
    out[...] = product[:pixels] * (1.0 / CODES)
    bias[...] = product[pixels:] * (1.0 / (CODES * band_pixels))


def invert(received, inverse, pixels, band_pixels):
    total_pairs, dates = inverse.shape[0], 2 * inverse.shape[1]
    return pl.pallas_call(
        partial(invert_kernel, band_pixels),
        in_specs=[pl.BlockSpec(memory_space=pltpu.VMEM)] * 2,
        out_specs=[pl.BlockSpec(memory_space=pltpu.VMEM)] * 2,
        out_shape=[
            jax.ShapeDtypeStruct((pixels, dates), jnp.float32),
            jax.ShapeDtypeStruct((8, dates), jnp.float32),
        ],
        scratch_shapes=[
            pltpu.VMEM((pixels + 8, total_pairs), jnp.float32),
            pltpu.VMEM((total_pairs, dates), jnp.float32),
        ],
        compiler_params=pltpu.CompilerParams(vmem_limit_bytes=24 << 20),
        name="invert",
    )(received, inverse)


def body(acquisitions, date_pairs, cycle_maps, inverse):
    group, _, height, width = acquisitions.shape
    devices = lax.axis_size("date")
    total_dates = group * devices
    pair_count, look_rows, look_cols = cycle_maps.shape
    rows = height // 2
    half = look_rows // 2
    me = lax.axis_index("date")
    odd = me % 2

    gaps = (date_pairs[:, 1] - date_pairs[:, 0] + total_dates) % total_dates
    combos = (date_pairs[:, 0] - me * group) * group + gaps - 1
    named = jnp.broadcast_to(combos[None, :, None], (1, half, look_cols))
    low_data = jnp.concatenate([cycle_maps[:, half:], named]).astype(jnp.bfloat16)
    words, exponent = coded_inverse(inverse)
    line = exponent_line(exponent)
    low_data, words = lax.optimization_barrier((low_data, words))
    low_data = passed_along(low_data, "date", 1)
    share = sent_inverse(words)

    def part(images, block, start, stop):
        return lax.dynamic_slice(images, (0, 0, block * rows, start), (group, 2, rows, stop - start))

    across = [(at, (at + 1 if at % 2 else at - 1) % devices) for at in range(devices)]
    groups = [[at, at + 1] for at in range(0, devices, 2)]
    beside, across_parts, left = [], [], acquisitions
    for start, stop in INNER:
        sent, left = lax.optimization_barrier((part(left, 1 - odd, start, stop), left))
        beside.append(lax.all_gather(sent, "date", axis_index_groups=groups))
    across_parts = [part(left, odd, start, stop) for start, stop in OUTER]
    across_parts, low_data = lax.optimization_barrier((across_parts, low_data))
    crossed = [lax.ppermute(sent, "date", across) for sent in across_parts]

    low_combos = low_data[-1, :, 0].astype(jnp.int32)
    cycles = jnp.stack([cycle_maps[:, :half].astype(jnp.float32), low_data[:-1].astype(jnp.float32)])
    cycles = (TWO_PI * cycles).reshape(2 * pair_count * half, look_cols).T

    inner = jnp.stack([odd, odd, odd * group, 1 - odd])
    outer = jnp.stack([1 - odd, 1 - odd, (1 - odd) * group, odd * 0])
    inner = jnp.concatenate([inner, jnp.where(odd == 0, combos, low_combos)])
    outer = jnp.concatenate([outer, jnp.where(odd == 0, low_combos, combos)])

    inverse = lax.all_gather(share, "row", axis=0, tiled=True).reshape(-1, LANES)

    earlier = ()
    for at, slot in ORDER:
        start, stop = (INNER, OUTER)[slot][at]
        other = crossed[at][None] if slot else beside[at]
        earlier = phases(
            slot,
            start,
            stop,
            (at, slot) == ORDER[-1],
            outer if slot else inner,
            acquisitions,
            other,
            cycles,
            line,
            earlier,
        )

    payload = earlier[0]
    received = lax.all_to_all(
        payload.reshape(devices, 1, -1), "date", split_axis=0, concat_axis=0, tiled=True
    ).reshape(payload.shape)
    out_cols = look_cols // devices
    row_count = lax.axis_size("row")
    result, bias = invert(received, inverse, out_cols * look_rows, look_rows * look_cols * row_count)
    for step in range(1, row_count):
        result = result - passed_along(bias, "row", step)[:1]
    result = result - bias[:1]
    return result.reshape(out_cols, look_rows, total_dates)


def solution(mesh):
    return jax.shard_map(
        body,
        mesh=mesh,
        in_specs=(
            P("date", None, "row", None),
            P("date", None),
            P("date", "row", None),
            P(None, "date"),
        ),
        out_specs=P("date", "row", None),
        check_vma=False,
    )
```

```python
from functools import partial
import math

import jax
import jax.numpy as jnp
from jax import lax
from jax.experimental import pallas as pl
from jax.experimental.pallas import tpu as pltpu
from jax.sharding import PartitionSpec as P

LOOK_R = 4
LOOK_C = 16
TWO_PI = 2.0 * math.pi
CODES = 32767.0 / TWO_PI
CHUNKS = ((0, 1024), (1024, 2048))
STEP = 512
MESSAGE = 8
LANES = 128


def passed_along(value, axis, steps):
    count = lax.axis_size(axis)
    pairs = [(source, (source + steps) % count) for source in range(count)]
    return lax.ppermute(value, axis, pairs)


def phase_kernel(slot, first_step, steps, final, scalars, own, other, cycles, *rest):
    payload, sums, images, products, high, low, words = rest[-7:]
    rest = rest[:-7]
    group, _, rows, width = own.shape
    looks = rows // LOOK_R
    pair_count = group * group
    out_cols = width // LOOK_C
    tiles = width // LANES
    sets = looks // 8
    half, own_at = scalars[0], scalars[2]
    step_at = pl.program_id(0)

    @pl.when(step_at == 0)
    def _():
        if len(rest) > 1:
            payload[...] = rest[1][...]
            sums[...] = rest[2][...]
        else:
            sums[...] = jnp.zeros_like(sums)

    @pl.loop(0, 2 * group)
    def _(index):
        date, part = index // 2, index % 2
        for source, start in ((own, own_at), (other, group - own_at)):
            for tile in range(tiles):
                images[start + date, part, tile] = source[
                    date, part, :, tile * LANES : (tile + 1) * LANES
                ].astype(jnp.float32)

    @pl.loop(0, tiles * sets)
    def _(index):
        tile, block = index // sets, index % sets
        real, imag = [None] * pair_count, [None] * pair_count
        for step in range(LOOK_R):
            at = pl.ds(block * 8 * LOOK_R + step, 8, stride=LOOK_R)
            parts = [[images[date, part, tile, at, :] for part in range(2)] for date in range(2 * group)]
            for date in range(group):
                a0, a1 = parts[date]
                for gap in range(group):
                    b0, b1 = parts[date + gap + 1]
                    combo = date * group + gap
                    re, im = a0 * b0 + a1 * b1, a1 * b0 - a0 * b1
                    real[combo] = re if step == 0 else real[combo] + re
                    imag[combo] = im if step == 0 else imag[combo] + im
        place = pl.ds(pl.multiple_of(block * 8, 8), 8)
        for combo in range(pair_count):
            products[combo, 0, tile, place, :] = real[combo]
            products[combo, 1, tile, place, :] = imag[combo]

    @pl.loop(0, pair_count)
    def _(pair):
        combo = scalars[4 + pair]
        for part in range(2):
            place = pl.ds(pl.multiple_of((part * pair_count + pair) * looks, 16), looks)
            for tile in range(tiles):
                value = products[combo, part, tile]
                head = value.astype(jnp.bfloat16)
                high[place, tile * LANES : (tile + 1) * LANES] = head
                low[place, tile * LANES : (tile + 1) * LANES] = (value - head.astype(jnp.float32)).astype(
                    jnp.bfloat16
                )

    shape = (out_cols, width)
    picked = lax.broadcasted_iota(jnp.int32, shape, 1) // LOOK_C == lax.broadcasted_iota(jnp.int32, shape, 0)
    picked = jnp.where(picked, 1.0, 0.0).astype(jnp.bfloat16)
    turned = (((1,), (1,)), ((), ()))
    looked = lax.dot_general(picked, high[...], turned, preferred_element_type=jnp.float32)
    looked += lax.dot_general(picked, low[...], turned, preferred_element_type=jnp.float32)
    half_width = looked.shape[1] // 2
    real, imag = looked[:, :half_width], looked[:, half_width:]
    imag = jnp.where(imag == 0.0, 0.0, imag)
    phase = jnp.arctan2(imag, real) - cycles[...]
    codes = jnp.round((phase + math.pi) * CODES)
    total = jnp.sum(codes, axis=0, keepdims=True).astype(jnp.int32)
    codes = codes.astype(jnp.int32)
    for octet in range(2):
        row = 2 * slot + octet
        sums[row : row + 1, :] += total[:, octet * LANES : (octet + 1) * LANES]
    words[...] = (codes[:, :LANES] << 16) | (codes[:, LANES:] & 0xFFFF)
    base = (step_at + first_step) * (out_cols // 2) * MESSAGE
    for col in range(2):
        place = pl.ds(base + 2 * col + half, out_cols // 2, stride=MESSAGE)
        payload[place, :] = words[pl.ds(col, out_cols // 2, stride=2), :]

    if final:

        @pl.when(step_at == steps - 1)
        def _():
            total = sums[...]
            for step in (8, 4, 2, 1):
                total += pltpu.roll(total, LANES - step, 1)
            lane = lax.broadcasted_iota(jnp.int32, (1, LANES), 1) % looks
            line = rest[0][0:1, :]
            for at in range(2):
                of = half if at == slot else 1 - half
                for octet in range(2):
                    row = 2 * at + octet
                    for side in range(2):
                        lanes_at = 2 * side + octet
                        moved = pltpu.roll(total, lanes_at, 1)[row : row + 1]
                        line = jnp.where((lane == lanes_at) & (of == side), moved, line)
            count = payload.shape[0] // MESSAGE
            payload[pl.ds(4, count, stride=MESSAGE), :] = jnp.broadcast_to(line, (count, LANES))


def phases(slot, start, stop, final, scalars, acquisitions, other, cycles, line, earlier):
    group, _, height, width = acquisitions.shape
    rows = height // 2
    first_step, steps = start // STEP, (stop - start) // STEP
    lanes = cycles.shape[1] // 2
    out_cols = STEP // LOOK_C
    payload_shape = (cycles.shape[0] // 2 * MESSAGE, LANES)
    looks = rows // LOOK_R
    tiles = STEP // LANES

    in_specs = [
        pl.BlockSpec((group, 2, rows, STEP), lambda i, p: (0, 0, p[1], first_step + i)),
        pl.BlockSpec((group, 2, rows, STEP), lambda i, p: (0, 0, 0, i)),
        pl.BlockSpec((out_cols, lanes), lambda i, p: (first_step + i, p[0])),
        pl.BlockSpec((8, LANES), lambda i, p: (0, 0)),
    ]
    outs = [
        pl.BlockSpec(payload_shape, lambda i, p: (0, 0)),
        pl.BlockSpec((8, LANES), lambda i, p: (0, 0)),
    ]
    return pl.pallas_call(
        partial(phase_kernel, slot, first_step, steps, final),
        grid_spec=pltpu.PrefetchScalarGridSpec(
            num_scalar_prefetch=1,
            grid=(steps,),
            in_specs=in_specs + outs[: len(earlier)],
            out_specs=outs,
            scratch_shapes=[
                pltpu.VMEM((2 * group, 2, tiles, rows, LANES), jnp.float32),
                pltpu.VMEM((group * group, 2, tiles, looks, LANES), jnp.float32),
                pltpu.VMEM((2 * lanes, STEP), jnp.bfloat16),
                pltpu.VMEM((2 * lanes, STEP), jnp.bfloat16),
                pltpu.VMEM((out_cols, LANES), jnp.int32),
            ],
        ),
        out_shape=[
            jax.ShapeDtypeStruct(payload_shape, jnp.int32),
            jax.ShapeDtypeStruct((8, LANES), jnp.int32),
        ],
        compiler_params=pltpu.CompilerParams(vmem_limit_bytes=20 << 20),
        cost_estimate=pl.CostEstimate(
            flops=8 * group * group * rows * (stop - start),
            bytes_accessed=group * 4 * rows * (stop - start) * 2,
            transcendentals=0,
        ),
        name="phases",
    )(scalars, acquisitions, other, cycles, line, *earlier)


def coded_inverse(inverse):
    turned = inverse.T
    peak = jnp.max(jnp.abs(turned), axis=1, keepdims=True)
    exponent = jnp.clip(jnp.floor(jnp.log2(peak)) + 1.0, -100.0, 100.0)
    codes = jnp.round(turned * jnp.exp2(-exponent) * 32767.0).astype(jnp.int32)
    words = (codes[:, :LANES] << 16) | (codes[:, LANES:] & 0xFFFF)
    return words, exponent[:, 0].astype(jnp.int32)


def exponent_line(exponent):
    spread = exponent.reshape(2, -1).T
    spread = jnp.pad(spread, ((0, 0), (4, LANES // spread.shape[0] - 6)))
    return jnp.broadcast_to(spread.reshape(1, LANES), (8, LANES))


def sent_inverse(words):
    devices = lax.axis_size("date")
    sent = jnp.broadcast_to(words[None], (devices, *words.shape))
    got = lax.all_to_all(sent, "date", split_axis=0, concat_axis=0, tiled=True)
    return got.reshape(-1, LANES)


def invert_kernel(band_pixels, received, inverse, out, bias, left, right):
    pair_count = 16
    sources = inverse.shape[0] // pair_count
    looks = LANES * 2 // pair_count
    pixels = out.shape[0]

    def aligned(words, half):
        value = words.astype(jnp.float32)
        return (pltpu.roll(value, sources - 1, 0) if half else value).T

    for pair in range(pair_count):
        words = inverse[pl.ds(pair, sources, stride=pair_count), :]
        place = slice(pair * sources, (pair + 1) * sources)
        right[place, :LANES] = (words >> 16).astype(jnp.float32)
        right[place, LANES:] = ((words << 16) >> 16).astype(jnp.float32)
    line = received[pl.ds(4, sources, stride=MESSAGE), :]
    lines = aligned(line, 0), aligned(line, 1)
    scales = []
    for pair in range(pair_count):
        octet, at = pair // 8, pair % 8 * looks
        scales.append(jnp.exp2(lines[0][at + 4 + octet : at + 5 + octet]) * (1.0 / 32767.0))
        total = lines[0][at + octet : at + octet + 1] + lines[1][at + 2 + octet : at + 3 + octet]
        left[pixels:, pair * sources : (pair + 1) * sources] = jnp.broadcast_to(
            total * scales[pair], (left.shape[0] - pixels, sources)
        )
    for half in range(2):
        for col in range(pixels // (2 * looks)):
            words = received[pl.ds(col * 2 + half, sources, stride=MESSAGE), :]
            for octet, value in enumerate((words >> 16, (words << 16) >> 16)):
                turned = aligned(value, half)
                for at in range(8):
                    pair = octet * 8 + at
                    row = (col * 2 + half) * looks
                    left[row : row + looks, pair * sources : (pair + 1) * sources] = (
                        turned[at * looks : (at + 1) * looks] * scales[pair]
                    )
    product = jnp.dot(
        left[...], right[...], precision=lax.Precision.HIGHEST, preferred_element_type=jnp.float32
    )
    out[...] = product[:pixels] * (1.0 / CODES)
    bias[...] = product[pixels:] * (1.0 / (CODES * band_pixels))


def invert(received, inverse, pixels, band_pixels):
    total_pairs, dates = inverse.shape[0], 2 * inverse.shape[1]
    return pl.pallas_call(
        partial(invert_kernel, band_pixels),
        in_specs=[pl.BlockSpec(memory_space=pltpu.VMEM)] * 2,
        out_specs=[pl.BlockSpec(memory_space=pltpu.VMEM)] * 2,
        out_shape=[
            jax.ShapeDtypeStruct((pixels, dates), jnp.float32),
            jax.ShapeDtypeStruct((8, dates), jnp.float32),
        ],
        scratch_shapes=[
            pltpu.VMEM((pixels + 8, total_pairs), jnp.float32),
            pltpu.VMEM((total_pairs, dates), jnp.float32),
        ],
        compiler_params=pltpu.CompilerParams(vmem_limit_bytes=24 << 20),
        name="invert",
    )(received, inverse)


def body(acquisitions, date_pairs, cycle_maps, inverse):
    group, _, height, width = acquisitions.shape
    devices = lax.axis_size("date")
    total_dates = group * devices
    pair_count, look_rows, look_cols = cycle_maps.shape
    rows = height // 2
    half = look_rows // 2
    me = lax.axis_index("date")

    gaps = (date_pairs[:, 1] - date_pairs[:, 0] + total_dates) % total_dates
    combos = (date_pairs[:, 0] - me * group) * group + gaps - 1
    named = jnp.broadcast_to(combos[None, :, None], (1, half, look_cols))
    low_data = jnp.concatenate([cycle_maps[:, half:], named]).astype(jnp.bfloat16)
    words, exponent = coded_inverse(inverse)
    line = exponent_line(exponent)
    low_data, words = lax.optimization_barrier((low_data, words))
    low_data = passed_along(low_data, "date", 1)
    inverse = sent_inverse(words)

    others, left = [], acquisitions
    for start, stop in CHUNKS:
        parts = left[:, :, :rows, start:stop], left[:, :, rows:, start:stop]
        parts, left, low_data = lax.optimization_barrier((parts, left, low_data))
        others.append((passed_along(parts[0], "date", -1), passed_along(parts[1], "date", 1)))

    low_combos = low_data[-1, :, 0].astype(jnp.int32)
    cycles = jnp.stack([cycle_maps[:, :half].astype(jnp.float32), low_data[:-1].astype(jnp.float32)])
    cycles = (TWO_PI * cycles).reshape(2 * pair_count * half, look_cols).T

    scalars = [
        jnp.concatenate([jnp.array([side, side, side * group, 0], jnp.int32), named])
        for side, named in enumerate((combos, low_combos))
    ]
    earlier = ()
    for chunk, (start, stop) in enumerate(CHUNKS):
        for side in range(2):
            earlier = phases(
                side,
                start,
                stop,
                stop == width and side == 1,
                scalars[side],
                acquisitions,
                others[chunk][side],
                cycles,
                line,
                earlier,
            )

    payload = earlier[0]
    received = lax.all_to_all(
        payload.reshape(devices, MESSAGE, LANES), "date", split_axis=0, concat_axis=0, tiled=True
    ).reshape(payload.shape)
    out_cols = look_cols // devices
    row_count = lax.axis_size("row")
    result, bias = invert(received, inverse, out_cols * look_rows, look_rows * look_cols * row_count)
    for step in range(1, row_count):
        result = result - passed_along(bias, "row", step)[:1]
    result = result - bias[:1]
    return result.reshape(out_cols, look_rows, total_dates)


def solution(mesh):
    return jax.shard_map(
        body,
        mesh=mesh,
        in_specs=(
            P("date", None, "row", None),
            P("date", None),
            P("date", "row", None),
            P(None, "date"),
        ),
        out_specs=P("date", "row", None),
        check_vma=False,
    )
```

```python
from functools import partial
import math

import jax
import jax.numpy as jnp
from jax import lax
from jax.experimental import pallas as pl
from jax.experimental.pallas import tpu as pltpu
from jax.sharding import PartitionSpec as P

LOOK_R = 4
LOOK_C = 16
TWO_PI = 2.0 * math.pi
CODES = 32767.0 / TWO_PI
CHUNKS = ((0, 1536), (1536, 2048))
STEP = 512
MESSAGE = 8
LANES = 128


def passed_along(value, axis, steps):
    count = lax.axis_size(axis)
    pairs = [(source, (source + steps) % count) for source in range(count)]
    return lax.ppermute(value, axis, pairs)


def phase_kernel(first_col, last, combos, own, following, previous, high_cycles, low_cycles, line, *rest):
    payload, sums, images, high, low, looked, picked, cycles, words = rest[-9:]
    group, _, rows, _ = following.shape
    _, width, _ = picked.shape
    looks = rows // LOOK_R
    pair_count = group * group
    step_cols = width // LOOK_C
    tiles = width // LANES
    cols = last - first_col
    steps = cols // step_cols
    if len(rest) == 9:
        sums[...] = jnp.zeros_like(sums)
    else:
        payload[...] = rest[0][...]
        sums[...] = rest[1][...]
    cycles[0] = TWO_PI * high_cycles[:, :looks, :].astype(jnp.float32).reshape(cycles.shape[1:])
    cycles[1] = TWO_PI * low_cycles[...].astype(jnp.float32).reshape(cycles.shape[1:])
    for step in range(steps):
        shape = picked.shape[1:]
        of = lax.broadcasted_iota(jnp.int32, shape, 0) // LOOK_C + first_col + step * step_cols
        chosen = of == lax.broadcasted_iota(jnp.int32, shape, 1)
        picked[step] = jnp.where(chosen, 1.0, 0.0).astype(jnp.bfloat16)

    def widen(source, start, row, col):
        @pl.loop(0, 2 * group)
        def _(index):
            date, part = index // 2, index % 2
            for tile in range(tiles):
                lanes = pl.ds(pl.multiple_of(col + tile * LANES, LANES), LANES)
                images[start + date, part, tile] = source[date, part, pl.ds(row, rows), lanes].astype(jnp.float32)

    @pl.loop(0, 2 * steps)
    def _(index):
        half, step_at = index // steps, index % steps
        widen(own, half * group, pl.multiple_of(half * rows, rows), step_at * width)

        @pl.when(half == 0)
        def _():
            widen(following, group, 0, step_at * width)

        @pl.when(half == 1)
        def _():
            widen(previous, 0, 0, step_at * width)

        @pl.loop(0, tiles)
        def _(tile):
            lanes = pl.ds(pl.multiple_of(tile * LANES, LANES), LANES)
            for date in range(0, group, 2):
                totals = {}
                for block in range(looks // 8):
                    for step in range(LOOK_R):
                        at = pl.ds(block * 8 * LOOK_R + step, 8, stride=LOOK_R)
                        seen = {
                            image: [images[image, part, tile, at, :] for part in range(2)]
                            for image in range(date, date + group + 2)
                        }
                        for first in range(date, date + 2):
                            a0, a1 = seen[first]
                            for gap in range(group):
                                b0, b1 = seen[first + gap + 1]
                                re, im = a0 * b0 + a1 * b1, a1 * b0 - a0 * b1
                                for part, value in enumerate((re, im)):
                                    key = first, gap, part, block
                                    totals[key] = totals[key] + value if key in totals else value
                for first in range(date, date + 2):
                    for gap in range(group):
                        for part in range(2):
                            value = jnp.concatenate(
                                [totals[first, gap, part, block] for block in range(looks // 8)], axis=0
                            )
                            head = value.astype(jnp.bfloat16)
                            tail = (value - head.astype(jnp.float32)).astype(jnp.bfloat16)
                            start = (part * pair_count + first * group + gap) * looks
                            high[start : start + looks, lanes] = head
                            low[start : start + looks, lanes] = tail

        summed = jnp.dot(high[...], picked[step_at], preferred_element_type=jnp.float32)
        summed += jnp.dot(low[...], picked[step_at], preferred_element_type=jnp.float32)

        @pl.when(step_at == 0)
        def _():
            looked[half] = summed

        @pl.when(step_at > 0)
        def _():
            looked[half] += summed

    @pl.loop(0, 2)
    def _(half):
        taken = []
        for part in range(2):
            for pair in range(pair_count):
                start = (part * pair_count + combos[half * pair_count + pair]) * looks
                taken.append(looked[half, pl.ds(pl.multiple_of(start, 8), looks), :])
        real = jnp.concatenate(taken[:pair_count], axis=0)
        imag = jnp.concatenate(taken[pair_count:], axis=0)
        imag = jnp.where(imag == 0.0, 0.0, imag)
        phase = jnp.arctan2(imag, real) - cycles[half]
        codes = jnp.round((phase + math.pi) * CODES).T[first_col:last]
        total = jnp.sum(codes, axis=0, keepdims=True).astype(jnp.int32)
        codes = codes.astype(jnp.int32)
        for octet in range(2):
            sums[pl.ds(2 * half + octet, 1), :] += total[:, octet * LANES : (octet + 1) * LANES]
        words[...] = (codes[:, :LANES] << 16) | (codes[:, LANES:] & 0xFFFF)
        for col in range(2):
            place = pl.ds(first_col // 2 * MESSAGE + 2 * col + half, cols // 2, stride=MESSAGE)
            payload[place, :] = words[pl.ds(col, cols // 2, stride=2), :]

    if last * MESSAGE // 2 == payload.shape[0]:

        total = sums[...]
        for step in (8, 4, 2, 1):
            total += pltpu.roll(total, LANES - step, 1)
        lane = lax.broadcasted_iota(jnp.int32, (1, LANES), 1) % looks
        full = line[0:1, :]
        for row in range(4):
            moved = pltpu.roll(total, row, 1)[row : row + 1]
            full = jnp.where(lane == row, moved, full)
        count = payload.shape[0] // MESSAGE
        payload[pl.ds(4, count, stride=MESSAGE), :] = jnp.broadcast_to(full, (count, LANES))


def phases(start, stop, combos, own, following, previous, high_cycles, low_cycles, line, earlier):
    group, _, height, _ = own.shape
    rows = height // 2
    looked_cols = low_cycles.shape[2]
    payload_shape = (looked_cols // 2 * MESSAGE, LANES)
    looks = rows // LOOK_R
    tiles = STEP // LANES
    pair_count = group * group
    steps = (stop - start) // STEP
    vmem = pl.BlockSpec(memory_space=pltpu.VMEM)
    return pl.pallas_call(
        partial(phase_kernel, start // LOOK_C, stop // LOOK_C),
        in_specs=[pl.BlockSpec(memory_space=pltpu.SMEM)] + [vmem] * (6 + len(earlier)),
        out_specs=[vmem] * 2,
        out_shape=[
            jax.ShapeDtypeStruct(payload_shape, jnp.int32),
            jax.ShapeDtypeStruct((8, LANES), jnp.int32),
        ],
        scratch_shapes=[
            pltpu.VMEM((2 * group, 2, tiles, rows, LANES), jnp.float32),
            pltpu.VMEM((2 * pair_count * looks, STEP), jnp.bfloat16),
            pltpu.VMEM((2 * pair_count * looks, STEP), jnp.bfloat16),
            pltpu.VMEM((2, 2 * pair_count * looks, looked_cols), jnp.float32),
            pltpu.VMEM((steps, STEP, looked_cols), jnp.bfloat16),
            pltpu.VMEM((2, pair_count * looks, looked_cols), jnp.float32),
            pltpu.VMEM(((stop - start) // LOOK_C, LANES), jnp.int32),
        ],
        compiler_params=pltpu.CompilerParams(vmem_limit_bytes=16 << 20),
        cost_estimate=pl.CostEstimate(
            flops=8 * pair_count * height * (stop - start),
            bytes_accessed=group * 4 * height * (stop - start) * 2,
            transcendentals=0,
        ),
        name="phases",
    )(combos, own, following, previous, high_cycles, low_cycles, line, *earlier)


def coded_inverse(inverse):
    turned = inverse.T
    peak = jnp.max(jnp.abs(turned), axis=1, keepdims=True)
    exponent = jnp.clip(jnp.floor(jnp.log2(peak)) + 1.0, -100.0, 100.0)
    codes = jnp.round(turned * jnp.exp2(-exponent) * 32767.0).astype(jnp.int32)
    words = (codes[:, :LANES] << 16) | (codes[:, LANES:] & 0xFFFF)
    return words, exponent[:, 0].astype(jnp.int32)


def exponent_line(exponent):
    spread = exponent.reshape(2, -1).T
    spread = jnp.pad(spread, ((0, 0), (4, LANES // spread.shape[0] - 6)))
    return jnp.broadcast_to(spread.reshape(1, LANES), (8, LANES))


def sent_inverse(words):
    devices = lax.axis_size("date")
    per = words.shape[0] // 2
    sent = jnp.broadcast_to(words.reshape(1, 2, per, LANES), (devices // 2, 2, per, LANES))
    got = lax.all_to_all(
        sent.reshape(devices, per, LANES), "date", split_axis=0, concat_axis=0, tiled=True
    ).reshape(-1, LANES)
    return got


def unpack_kernel(side, kept, swapped, right):
    pair_count = 16
    per = pair_count // 2
    sources = kept.shape[0] // per
    for at in range(per):
        for owner, source in ((side[0], kept), (1 - side[0], swapped)):
            words = source[pl.ds(at, sources, stride=per), :]
            place = pl.ds(pl.multiple_of((owner * per + at) * sources, 8), sources)
            right[place, :LANES] = (words >> 16).astype(jnp.float32)
            right[place, LANES:] = ((words << 16) >> 16).astype(jnp.float32)


def unpacked(kept, swapped):
    vmem = pl.BlockSpec(memory_space=pltpu.VMEM)
    return pl.pallas_call(
        unpack_kernel,
        in_specs=[pl.BlockSpec(memory_space=pltpu.SMEM), vmem, vmem],
        out_specs=vmem,
        out_shape=jax.ShapeDtypeStruct((2 * kept.shape[0], 2 * LANES), jnp.float32),
        name="unpack",
    )((lax.axis_index("date") % 2).reshape(1), kept, swapped)


def invert_kernel(band_pixels, received, right, out, bias, left):
    pair_count = 16
    sources = right.shape[0] // pair_count
    looks = LANES * 2 // pair_count
    pixels = out.shape[0]

    def aligned(words, half):
        value = words.astype(jnp.float32)
        return (pltpu.roll(value, sources - 1, 0) if half else value).T

    line = received[pl.ds(4, sources, stride=MESSAGE), :]
    lines = aligned(line, 0), aligned(line, 1)
    scales = []
    for pair in range(pair_count):
        octet, at = pair // 8, pair % 8 * looks
        scales.append(jnp.exp2(lines[0][at + 4 + octet : at + 5 + octet]) * (1.0 / 32767.0))
        total = lines[0][at + octet : at + octet + 1] + lines[1][at + 2 + octet : at + 3 + octet]
        left[pixels:, pair * sources : (pair + 1) * sources] = jnp.broadcast_to(
            total * scales[pair], (left.shape[0] - pixels, sources)
        )
    for half in range(2):
        for col in range(pixels // (2 * looks)):
            words = received[pl.ds(col * 2 + half, sources, stride=MESSAGE), :]
            for octet, value in enumerate((words >> 16, (words << 16) >> 16)):
                turned = aligned(value, half)
                for at in range(8):
                    pair = octet * 8 + at
                    row = (col * 2 + half) * looks
                    left[row : row + looks, pair * sources : (pair + 1) * sources] = (
                        turned[at * looks : (at + 1) * looks] * scales[pair]
                    )
    product = jnp.dot(
        left[...], right[...], precision=lax.Precision.HIGHEST, preferred_element_type=jnp.float32
    )
    out[...] = product[:pixels] * (1.0 / CODES)
    bias[...] = product[pixels:] * (1.0 / (CODES * band_pixels))


def invert(received, codes, pixels, band_pixels):
    total_pairs, dates = codes.shape
    vmem = pl.BlockSpec(memory_space=pltpu.VMEM)
    return pl.pallas_call(
        partial(invert_kernel, band_pixels),
        in_specs=[vmem] * 2,
        out_specs=[vmem] * 2,
        out_shape=[
            jax.ShapeDtypeStruct((pixels, dates), jnp.float32),
            jax.ShapeDtypeStruct((8, dates), jnp.float32),
        ],
        scratch_shapes=[pltpu.VMEM((pixels + 8, total_pairs), jnp.float32)],
        compiler_params=pltpu.CompilerParams(vmem_limit_bytes=24 << 20),
        name="invert",
    )(received, codes)


def body(acquisitions, date_pairs, cycle_maps, inverse):
    group, _, height, width = acquisitions.shape
    devices = lax.axis_size("date")
    total_dates = group * devices
    pair_count, look_rows, look_cols = cycle_maps.shape
    rows = height // 2
    half = look_rows // 2
    me = lax.axis_index("date")

    def parts(images, start, stop):
        return images[:, :, :rows, start:stop], images[:, :, rows:, start:stop]

    def exchanged(pair):
        return passed_along(pair[0], "date", -1), passed_along(pair[1], "date", 1)

    gaps = (date_pairs[:, 1] - date_pairs[:, 0] + total_dates) % total_dates
    combos = (date_pairs[:, 0] - me * group) * group + gaps - 1
    low_combos = passed_along(combos, "date", 1)
    low_cycles = passed_along(cycle_maps[:, half:].astype(jnp.bfloat16), "date", 1)
    left, others = acquisitions, []
    for start, stop in CHUNKS:
        sent, left, low_combos, low_cycles, inverse = lax.optimization_barrier(
            (parts(left, start, stop), left, low_combos, low_cycles, inverse)
        )
        others.append(exchanged(sent))

    words, exponent = coded_inverse(inverse)
    line = exponent_line(exponent)
    kept = sent_inverse(words)

    combos = jnp.concatenate([combos, low_combos])
    owned = [acquisitions[:, :, :, start:stop] for start, stop in CHUNKS]
    owned, combos = lax.optimization_barrier((owned, combos))
    earlier = ()
    for (start, stop), own, (following, previous) in zip(CHUNKS, owned, others):
        blank = jnp.zeros_like(line) if stop < width else line
        earlier = phases(
            start, stop, combos, own, following, previous, cycle_maps, low_cycles, blank, earlier
        )

    payload, kept = lax.optimization_barrier((earlier[0], kept))
    swapped = lax.ppermute(kept, "date", [(at, at ^ 1) for at in range(devices)])
    codes = unpacked(kept, swapped)
    received = lax.all_to_all(
        payload.reshape(devices, MESSAGE, LANES), "date", split_axis=0, concat_axis=0, tiled=True
    ).reshape(payload.shape)
    out_cols = look_cols // devices
    row_count = lax.axis_size("row")
    result, bias = invert(received, codes, out_cols * look_rows, look_rows * look_cols * row_count)
    for step in range(1, row_count):
        result = result - passed_along(bias, "row", step)[:1]
    result = result - bias[:1]
    return result.reshape(out_cols, look_rows, total_dates)


def solution(mesh):
    return jax.shard_map(
        body,
        mesh=mesh,
        in_specs=(
            P("date", None, "row", None),
            P("date", None),
            P("date", "row", None),
            P(None, "date"),
        ),
        out_specs=P("date", "row", None),
        check_vma=False,
    )
```

```python
from functools import partial
import math

import jax
import jax.numpy as jnp
from jax import lax
from jax.experimental import pallas as pl
from jax.experimental.pallas import tpu as pltpu
from jax.sharding import PartitionSpec as P

LOOK_R = 4
LOOK_C = 16
TWO_PI = 2.0 * math.pi
CODES = 32767.0 / TWO_PI
CHUNKS = ((0, 1536), (1536, 2048))
STEP = 512
MESSAGE = 5
LANES = 128
ATAN = (
    0.9999993329,
    -0.3332985605,
    0.1994653599,
    -0.1390853351,
    0.0964200441,
    -0.0559098861,
    0.0218612288,
    -0.0040540580,
)


def passed_along(value, axis, steps):
    count = lax.axis_size(axis)
    pairs = [(source, (source + steps) % count) for source in range(count)]
    return lax.ppermute(value, axis, pairs)


def arctan2(y, x):
    wide, tall = jnp.abs(x), jnp.abs(y)
    larger = jnp.maximum(wide, tall)
    ratio = jnp.minimum(wide, tall) / jnp.where(larger == 0.0, 1.0, larger)
    square = ratio * ratio
    value = jnp.full_like(square, ATAN[-1])
    for factor in ATAN[-2::-1]:
        value = value * square + factor
    value = value * ratio
    value = jnp.where(tall > wide, 0.5 * math.pi - value, value)
    value = jnp.where(x < 0.0, math.pi - value, value)
    return jnp.where(y < 0.0, -value, value)


def phase_kernel(first_col, last, final, own, following, previous, *refs):
    refs = list(refs)
    earlier = refs.pop(0) if first_col else None
    if final:
        combos, high_cycles, low_cycles, line, payload, images, high, low, picked, looked, cycles, sums, words = refs
    else:
        looked, images, high, low, picked = refs
    group, _, rows, _ = following.shape
    steps, width, _ = picked.shape
    looks = rows // LOOK_R
    pair_count = group * group
    step_cols = width // LOOK_C
    tiles = width // LANES
    for step in range(steps):
        shape = picked.shape[1:]
        of = lax.broadcasted_iota(jnp.int32, shape, 0) // LOOK_C + first_col + step * step_cols
        chosen = of == lax.broadcasted_iota(jnp.int32, shape, 1)
        picked[step] = jnp.where(chosen, 1.0, 0.0).astype(jnp.bfloat16)

    def widen(source, start, row, col):
        @pl.loop(0, 2 * group)
        def _(index):
            date, part = index // 2, index % 2
            for tile in range(tiles):
                lanes = pl.ds(pl.multiple_of(col + tile * LANES, LANES), LANES)
                images[start + date, part, tile] = source[date, part, pl.ds(row, rows), lanes].astype(jnp.float32)

    @pl.loop(0, 2 * steps)
    def _(index):
        half, step_at = index // steps, index % steps
        widen(own, half * group, pl.multiple_of(half * rows, rows), first_col * LOOK_C + step_at * width)

        @pl.when(half == 0)
        def _():
            widen(following, group, 0, step_at * width)

        @pl.when(half == 1)
        def _():
            widen(previous, 0, 0, step_at * width)

        @pl.loop(0, tiles)
        def _(tile):
            lanes = pl.ds(pl.multiple_of(tile * LANES, LANES), LANES)
            for date in range(0, group, 2):
                totals = {}
                for block in range(looks // 8):
                    for step in range(LOOK_R):
                        at = pl.ds(block * 8 * LOOK_R + step, 8, stride=LOOK_R)
                        seen = {
                            image: [images[image, part, tile, at, :] for part in range(2)]
                            for image in range(date, date + group + 2)
                        }
                        for first in range(date, date + 2):
                            a0, a1 = seen[first]
                            for gap in range(group):
                                b0, b1 = seen[first + gap + 1]
                                re, im = a0 * b0 + a1 * b1, a1 * b0 - a0 * b1
                                for part, value in enumerate((re, im)):
                                    key = first, gap, part, block
                                    totals[key] = totals[key] + value if key in totals else value
                for first in range(date, date + 2):
                    for gap in range(group):
                        for part in range(2):
                            value = jnp.concatenate(
                                [totals[first, gap, part, block] for block in range(looks // 8)], axis=0
                            )
                            head = value.astype(jnp.bfloat16)
                            tail = (value - head.astype(jnp.float32)).astype(jnp.bfloat16)
                            start = (part * pair_count + first * group + gap) * looks
                            high[start : start + looks, lanes] = head
                            low[start : start + looks, lanes] = tail

        summed = jnp.dot(high[...], picked[step_at], preferred_element_type=jnp.float32)
        summed += jnp.dot(low[...], picked[step_at], preferred_element_type=jnp.float32)

        @pl.when(step_at == 0)
        def _():
            looked[half] = summed if earlier is None else earlier[half] + summed

        @pl.when(step_at > 0)
        def _():
            looked[half] += summed

    if not final:
        return
    cycles[0] = TWO_PI * high_cycles[:, :looks, :].astype(jnp.float32).reshape(cycles.shape[1:])
    cycles[1] = TWO_PI * low_cycles[...].astype(jnp.float32).reshape(cycles.shape[1:])

    @pl.loop(0, 2)
    def _(half):
        taken = []
        for part in range(2):
            for pair in range(pair_count):
                start = (part * pair_count + combos[half * pair_count + pair]) * looks
                taken.append(looked[half, pl.ds(pl.multiple_of(start, 8), looks), :])
        real = jnp.concatenate(taken[:pair_count], axis=0)
        imag = jnp.concatenate(taken[pair_count:], axis=0)
        codes = jnp.round((arctan2(imag, real) - cycles[half] + math.pi) * CODES).T
        total = jnp.sum(codes, axis=0, keepdims=True).astype(jnp.int32)
        codes = codes.astype(jnp.int32)
        for octet in range(2):
            sums[pl.ds(2 * half + octet, 1), :] = total[:, octet * LANES : (octet + 1) * LANES]
        words[...] = (codes[:, :LANES] << 16) | (codes[:, LANES:] & 0xFFFF)
        count = last // 2
        for col in range(2):
            payload[pl.ds(2 * col + half, count, stride=MESSAGE), :] = words[pl.ds(col, count, stride=2), :]

    total = sums[...]
    for step in (8, 4, 2, 1):
        total += pltpu.roll(total, LANES - step, 1)
    lane = lax.broadcasted_iota(jnp.int32, (1, LANES), 1) % looks
    full = line[0:1, :]
    for row in range(4):
        moved = pltpu.roll(total, row, 1)[row : row + 1]
        full = jnp.where(lane == row, moved, full)
    payload[pl.ds(4, last // 2, stride=MESSAGE), :] = jnp.broadcast_to(full, (last // 2, LANES))


def phases(start, stop, final, own, following, previous, earlier, *rest):
    group, _, height, _ = own.shape
    rows = height // 2
    looked_cols = own.shape[3] // LOOK_C
    looks = rows // LOOK_R
    tiles = STEP // LANES
    pair_count = group * group
    steps = (stop - start) // STEP
    vmem = pl.BlockSpec(memory_space=pltpu.VMEM)
    in_specs = [vmem] * (3 + len(earlier))
    looked_shape = (2, 2 * pair_count * looks, looked_cols)
    out_shape = jax.ShapeDtypeStruct(looked_shape, jnp.float32)
    scratch = [
        pltpu.VMEM((2 * group, 2, tiles, rows, LANES), jnp.float32),
        pltpu.VMEM((2 * pair_count * looks, STEP), jnp.bfloat16),
        pltpu.VMEM((2 * pair_count * looks, STEP), jnp.bfloat16),
        pltpu.VMEM((steps, STEP, looked_cols), jnp.bfloat16),
    ]
    if final:
        in_specs += [pl.BlockSpec(memory_space=pltpu.SMEM)] + [vmem] * 3
        out_shape = jax.ShapeDtypeStruct((looked_cols // 2 * MESSAGE, LANES), jnp.int32)
        scratch += [
            pltpu.VMEM(looked_shape, jnp.float32),
            pltpu.VMEM((2, pair_count * looks, looked_cols), jnp.float32),
            pltpu.VMEM((8, LANES), jnp.int32),
            pltpu.VMEM((looked_cols, LANES), jnp.int32),
        ]
    return pl.pallas_call(
        partial(phase_kernel, start // LOOK_C, stop // LOOK_C, final),
        in_specs=in_specs,
        out_specs=vmem,
        out_shape=out_shape,
        scratch_shapes=scratch,
        compiler_params=pltpu.CompilerParams(vmem_limit_bytes=16 << 20),
        cost_estimate=pl.CostEstimate(
            flops=8 * pair_count * height * (stop - start),
            bytes_accessed=group * 4 * height * (stop - start) * 2,
            transcendentals=0,
        ),
        name="phases",
    )(own, following, previous, *earlier, *rest)


def coded_inverse(inverse):
    turned = inverse.T
    peak = jnp.max(jnp.abs(turned), axis=1, keepdims=True)
    exponent = jnp.clip(jnp.floor(jnp.log2(peak)) + 1.0, -100.0, 100.0)
    codes = jnp.round(turned * jnp.exp2(-exponent) * 32767.0).astype(jnp.int32)
    words = (codes[:, :LANES] << 16) | (codes[:, LANES:] & 0xFFFF)
    return words, exponent[:, 0].astype(jnp.int32)


def exponent_line(exponent):
    spread = exponent.reshape(2, -1).T
    spread = jnp.pad(spread, ((0, 0), (4, LANES // spread.shape[0] - 6)))
    return jnp.broadcast_to(spread.reshape(1, LANES), (8, LANES))


def sent_inverse(words):
    devices = lax.axis_size("date")
    per = words.shape[0] // 2
    sent = jnp.broadcast_to(words.reshape(1, 2, per, LANES), (devices // 2, 2, per, LANES))
    got = lax.all_to_all(
        sent.reshape(devices, per, LANES), "date", split_axis=0, concat_axis=0, tiled=True
    ).reshape(-1, LANES)
    return got


def invert_kernel(band_pixels, side, received, kept, swapped, out, bias, left, right):
    pair_count = 16
    per = pair_count // 2
    sources = kept.shape[0] // per
    looks = LANES * 2 // pair_count
    pixels = out.shape[0]

    def aligned(words, half):
        value = words.astype(jnp.float32)
        return (pltpu.roll(value, sources - 1, 0) if half else value).T

    for at in range(per):
        for owner, source in ((side[0], kept), (1 - side[0], swapped)):
            words = source[pl.ds(at, sources, stride=per), :]
            place = pl.ds(pl.multiple_of((owner * per + at) * sources, 8), sources)
            right[place, :LANES] = (words >> 16).astype(jnp.float32)
            right[place, LANES:] = ((words << 16) >> 16).astype(jnp.float32)
    line = received[pl.ds(4, sources, stride=MESSAGE), :]
    lines = aligned(line, 0), aligned(line, 1)
    scales = []
    for pair in range(pair_count):
        octet, at = pair // 8, pair % 8 * looks
        scales.append(jnp.exp2(lines[0][at + 4 + octet : at + 5 + octet]) * (1.0 / 32767.0))
        total = lines[0][at + octet : at + octet + 1] + lines[1][at + 2 + octet : at + 3 + octet]
        left[pixels:, pair * sources : (pair + 1) * sources] = jnp.broadcast_to(
            total * scales[pair], (left.shape[0] - pixels, sources)
        )
    for half in range(2):
        for col in range(pixels // (2 * looks)):
            words = received[pl.ds(col * 2 + half, sources, stride=MESSAGE), :]
            for octet, value in enumerate((words >> 16, (words << 16) >> 16)):
                turned = aligned(value, half)
                for at in range(8):
                    pair = octet * 8 + at
                    row = (col * 2 + half) * looks
                    left[row : row + looks, pair * sources : (pair + 1) * sources] = (
                        turned[at * looks : (at + 1) * looks] * scales[pair]
                    )
    product = jnp.dot(
        left[...], right[...], precision=lax.Precision.HIGHEST, preferred_element_type=jnp.float32
    )
    out[...] = product[:pixels] * (1.0 / CODES)
    bias[...] = product[pixels:] * (1.0 / (CODES * band_pixels))


def invert(received, kept, swapped, pixels, band_pixels):
    total_pairs, dates = 2 * kept.shape[0], 2 * LANES
    vmem = pl.BlockSpec(memory_space=pltpu.VMEM)
    return pl.pallas_call(
        partial(invert_kernel, band_pixels),
        in_specs=[pl.BlockSpec(memory_space=pltpu.SMEM)] + [vmem] * 3,
        out_specs=[vmem] * 2,
        out_shape=[
            jax.ShapeDtypeStruct((pixels, dates), jnp.float32),
            jax.ShapeDtypeStruct((8, dates), jnp.float32),
        ],
        scratch_shapes=[
            pltpu.VMEM((pixels + 8, total_pairs), jnp.float32),
            pltpu.VMEM((total_pairs, dates), jnp.float32),
        ],
        compiler_params=pltpu.CompilerParams(vmem_limit_bytes=16 << 20),
        name="invert",
    )((lax.axis_index("date") % 2).reshape(1), received, kept, swapped)


def body(acquisitions, date_pairs, cycle_maps, inverse):
    group, _, height, width = acquisitions.shape
    devices = lax.axis_size("date")
    total_dates = group * devices
    pair_count, look_rows, look_cols = cycle_maps.shape
    rows = height // 2
    half = look_rows // 2
    me = lax.axis_index("date")

    def parts(images, start, stop):
        return images[:, :, :rows, start:stop], images[:, :, rows:, start:stop]

    def exchanged(pair):
        return passed_along(pair[0], "date", -1), passed_along(pair[1], "date", 1)

    gaps = (date_pairs[:, 1] - date_pairs[:, 0] + total_dates) % total_dates
    combos = (date_pairs[:, 0] - me * group) * group + gaps - 1
    low_combos = passed_along(combos, "date", 1)
    low_cycles = passed_along(cycle_maps[:, half:].astype(jnp.bfloat16), "date", 1)
    left, others = acquisitions, []
    for start, stop in CHUNKS:
        sent, left, low_combos, low_cycles, inverse = lax.optimization_barrier(
            (parts(left, start, stop), left, low_combos, low_cycles, inverse)
        )
        others.append(exchanged(sent))

    words, exponent = coded_inverse(inverse)
    line = exponent_line(exponent)
    kept = sent_inverse(words)

    combos = jnp.concatenate([combos, low_combos])
    looked = ()
    for (start, stop), (following, previous) in zip(CHUNKS, others):
        final = stop == width
        rest = (combos, cycle_maps, low_cycles, line) if final else ()
        looked = (phases(start, stop, final, acquisitions, following, previous, looked, *rest),)

    payload, kept = lax.optimization_barrier((looked[0], kept))
    swapped = lax.ppermute(kept, "date", [(at, at ^ 1) for at in range(devices)])
    received = lax.all_to_all(
        payload.reshape(devices, 1, -1), "date", split_axis=0, concat_axis=0, tiled=True
    ).reshape(payload.shape)
    out_cols = look_cols // devices
    row_count = lax.axis_size("row")
    result, bias = invert(received, kept, swapped, out_cols * look_rows, look_rows * look_cols * row_count)
    for step in range(1, row_count):
        result = result - passed_along(bias, "row", step)[:1]
    result = result - bias[:1]
    return result.reshape(out_cols, look_rows, total_dates)


def solution(mesh):
    return jax.shard_map(
        body,
        mesh=mesh,
        in_specs=(
            P("date", None, "row", None),
            P("date", None),
            P("date", "row", None),
            P(None, "date"),
        ),
        out_specs=P("date", "row", None),
        check_vma=False,
    )
```

```python
from functools import partial
import math

import jax
import jax.numpy as jnp
from jax import lax
from jax.experimental import pallas as pl
from jax.experimental.pallas import tpu as pltpu
from jax.sharding import PartitionSpec as P

LOOK_R = 4
LOOK_C = 16
TWO_PI = 2.0 * math.pi
CODES = 32767.0 / TWO_PI
CHUNKS = ((0, 1536), (1536, 2048))
STEP = 512
MESSAGE = 5
LANES = 128
ATAN = (
    0.9999993329,
    -0.3332985605,
    0.1994653599,
    -0.1390853351,
    0.0964200441,
    -0.0559098861,
    0.0218612288,
    -0.0040540580,
)


def passed_along(value, axis, steps):
    count = lax.axis_size(axis)
    pairs = [(source, (source + steps) % count) for source in range(count)]
    return lax.ppermute(value, axis, pairs)


def arctan2(y, x):
    wide, tall = jnp.abs(x), jnp.abs(y)
    larger = jnp.maximum(wide, tall)
    ratio = jnp.minimum(wide, tall) / jnp.where(larger == 0.0, 1.0, larger)
    square = ratio * ratio
    value = jnp.full_like(square, ATAN[-1])
    for factor in ATAN[-2::-1]:
        value = value * square + factor
    value = value * ratio
    value = jnp.where(tall > wide, 0.5 * math.pi - value, value)
    value = jnp.where(x < 0.0, math.pi - value, value)
    return jnp.where(y < 0.0, -value, value)


def phase_kernel(first_col, last, final, own, following, previous, *refs):
    refs = list(refs)
    earlier = refs.pop(0) if first_col else None
    if final:
        combos, high_cycles, low_cycles, line, payload, images, high, low, picked, looked, cycles, sums, words = refs
    else:
        looked, images, high, low, picked = refs
    group, _, rows, _ = following.shape
    steps, width, _ = picked.shape
    looks = rows // LOOK_R
    pair_count = group * group
    step_cols = width // LOOK_C
    tiles = width // LANES
    for step in range(steps):
        shape = picked.shape[1:]
        of = lax.broadcasted_iota(jnp.int32, shape, 0) // LOOK_C + first_col + step * step_cols
        chosen = of == lax.broadcasted_iota(jnp.int32, shape, 1)
        picked[step] = jnp.where(chosen, 1.0, 0.0).astype(jnp.bfloat16)

    def widen(source, start, row, col):
        @pl.loop(0, 2 * group)
        def _(index):
            date, part = index // 2, index % 2
            for tile in range(tiles):
                lanes = pl.ds(pl.multiple_of(col + tile * LANES, LANES), LANES)
                images[start + date, part, tile] = source[date, part, pl.ds(row, rows), lanes].astype(jnp.float32)

    looked[...] = jnp.zeros_like(looked) if earlier is None else earlier[...]
    quarter = high.shape[1] // tiles

    def multiplied(index, piece):
        place = pl.ds(pl.multiple_of(piece * quarter, quarter), quarter)
        chosen = picked[lax.rem(index + steps, steps)]
        held = lax.rem(index + 2, 2)
        summed = jnp.dot(high[held, place, :], chosen, preferred_element_type=jnp.float32)
        summed += jnp.dot(low[held, place, :], chosen, preferred_element_type=jnp.float32)
        target = jnp.where(index < 0, 2, index // steps)
        looked[target, place, :] += summed

    @pl.loop(0, 2 * steps)
    def _(index):
        half, step_at = index // steps, index % steps
        widen(own, half * group, pl.multiple_of(half * rows, rows), step_at * width)

        @pl.when(half == 0)
        def _():
            widen(following, group, 0, step_at * width)

        @pl.when(half == 1)
        def _():
            widen(previous, 0, 0, step_at * width)

        @pl.loop(0, tiles)
        def _(tile):
            multiplied(index - 1, tile)
            lanes = pl.ds(pl.multiple_of(tile * LANES, LANES), LANES)
            for date in range(0, group, 2):
                totals = {}
                for block in range(looks // 8):
                    for step in range(LOOK_R):
                        at = pl.ds(block * 8 * LOOK_R + step, 8, stride=LOOK_R)
                        seen = {
                            image: [images[image, part, tile, at, :] for part in range(2)]
                            for image in range(date, date + group + 2)
                        }
                        for first in range(date, date + 2):
                            a0, a1 = seen[first]
                            for gap in range(group):
                                b0, b1 = seen[first + gap + 1]
                                re, im = a0 * b0 + a1 * b1, a1 * b0 - a0 * b1
                                for part, value in enumerate((re, im)):
                                    key = first, gap, part, block
                                    totals[key] = totals[key] + value if key in totals else value
                for first in range(date, date + 2):
                    for gap in range(group):
                        for part in range(2):
                            value = jnp.concatenate(
                                [totals[first, gap, part, block] for block in range(looks // 8)], axis=0
                            )
                            head = value.astype(jnp.bfloat16)
                            tail = (value - head.astype(jnp.float32)).astype(jnp.bfloat16)
                            start = (part * pair_count + first * group + gap) * looks
                            high[lax.rem(index, 2), start : start + looks, lanes] = head
                            low[lax.rem(index, 2), start : start + looks, lanes] = tail

    @pl.loop(0, tiles)
    def _(piece):
        multiplied(2 * steps - 1, piece)

    if not final:
        return
    cycles[0] = TWO_PI * high_cycles[:, :looks, :].astype(jnp.float32).reshape(cycles.shape[1:])
    cycles[1] = TWO_PI * low_cycles[:, looks:, :].astype(jnp.float32).reshape(cycles.shape[1:])

    @pl.loop(0, 2)
    def _(half):
        taken = []
        for part in range(2):
            for pair in range(pair_count):
                start = (part * pair_count + combos[half * pair_count + pair]) * looks
                taken.append(looked[half, pl.ds(pl.multiple_of(start, 8), looks), :])
        real = jnp.concatenate(taken[:pair_count], axis=0)
        imag = jnp.concatenate(taken[pair_count:], axis=0)
        codes = jnp.round((arctan2(imag, real) - cycles[half] + math.pi) * CODES).T
        total = jnp.sum(codes, axis=0, keepdims=True).astype(jnp.int32)
        codes = codes.astype(jnp.int32)
        for octet in range(2):
            sums[pl.ds(2 * half + octet, 1), :] = total[:, octet * LANES : (octet + 1) * LANES]
        words[...] = (codes[:, :LANES] << 16) | (codes[:, LANES:] & 0xFFFF)
        count = last // 2
        for col in range(2):
            payload[pl.ds(2 * col + half, count, stride=MESSAGE), :] = words[pl.ds(col, count, stride=2), :]

    total = sums[...]
    for step in (8, 4, 2, 1):
        total += pltpu.roll(total, LANES - step, 1)
    lane = lax.broadcasted_iota(jnp.int32, (1, LANES), 1) % looks
    full = line[0:1, :]
    for row in range(4):
        moved = pltpu.roll(total, row, 1)[row : row + 1]
        full = jnp.where(lane == row, moved, full)
    payload[pl.ds(4, last // 2, stride=MESSAGE), :] = jnp.broadcast_to(full, (last // 2, LANES))


def phases(start, stop, final, own, following, previous, earlier, *rest):
    group, _, height, _ = own.shape
    rows = height // 2
    looked_cols = LANES
    looks = rows // LOOK_R
    tiles = STEP // LANES
    pair_count = group * group
    steps = (stop - start) // STEP
    vmem = pl.BlockSpec(memory_space=pltpu.VMEM)
    in_specs = [vmem] * (3 + len(earlier))
    looked_shape = (3, 2 * pair_count * looks, looked_cols)
    out_shape = jax.ShapeDtypeStruct(looked_shape, jnp.float32)
    scratch = [
        pltpu.VMEM((2 * group, 2, tiles, rows, LANES), jnp.float32),
        pltpu.VMEM((2, 2 * pair_count * looks, STEP), jnp.bfloat16),
        pltpu.VMEM((2, 2 * pair_count * looks, STEP), jnp.bfloat16),
        pltpu.VMEM((steps, STEP, looked_cols), jnp.bfloat16),
    ]
    if final:
        in_specs += [pl.BlockSpec(memory_space=pltpu.SMEM)] + [vmem] * 3
        out_shape = jax.ShapeDtypeStruct((looked_cols // 2 * MESSAGE, LANES), jnp.int32)
        scratch += [
            pltpu.VMEM(looked_shape, jnp.float32),
            pltpu.VMEM((2, pair_count * looks, looked_cols), jnp.float32),
            pltpu.VMEM((8, LANES), jnp.int32),
            pltpu.VMEM((looked_cols, LANES), jnp.int32),
        ]
    return pl.pallas_call(
        partial(phase_kernel, start // LOOK_C, stop // LOOK_C, final),
        in_specs=in_specs,
        out_specs=vmem,
        out_shape=out_shape,
        scratch_shapes=scratch,
        compiler_params=pltpu.CompilerParams(vmem_limit_bytes=16 << 20),
        cost_estimate=pl.CostEstimate(
            flops=8 * pair_count * height * (stop - start),
            bytes_accessed=group * 4 * height * (stop - start) * 2,
            transcendentals=0,
        ),
        name="phases",
    )(own, following, previous, *earlier, *rest)


def coded_inverse(inverse):
    turned = inverse.T
    peak = jnp.max(jnp.abs(turned), axis=1, keepdims=True)
    exponent = jnp.clip(jnp.floor(jnp.log2(peak)) + 1.0, -100.0, 100.0)
    codes = jnp.round(turned * jnp.exp2(-exponent) * 32767.0).astype(jnp.int32)
    words = (codes[:, :LANES] << 16) | (codes[:, LANES:] & 0xFFFF)
    return words, exponent[:, 0].astype(jnp.int32)


def exponent_line(exponent):
    spread = exponent.reshape(2, -1).T
    spread = jnp.pad(spread, ((0, 0), (4, LANES // spread.shape[0] - 6)))
    return jnp.broadcast_to(spread.reshape(1, LANES), (8, LANES))


def sent_inverse(words):
    devices = lax.axis_size("date")
    per = words.shape[0] // 2
    sent = jnp.broadcast_to(words.reshape(1, 2, per, LANES), (devices // 2, 2, per, LANES))
    got = lax.all_to_all(
        sent.reshape(devices, per, LANES), "date", split_axis=0, concat_axis=0, tiled=True
    ).reshape(-1, LANES)
    return got


def invert_kernel(band_pixels, side, received, kept, swapped, out, bias, left, right):
    pair_count = 16
    per = pair_count // 2
    sources = kept.shape[0] // per
    looks = LANES * 2 // pair_count
    pixels = out.shape[0]

    def aligned(words, half):
        value = words.astype(jnp.float32)
        return (pltpu.roll(value, sources - 1, 0) if half else value).T

    for at in range(per):
        for owner, source in ((side[0], kept), (1 - side[0], swapped)):
            words = source[pl.ds(at, sources, stride=per), :]
            place = pl.ds(pl.multiple_of((owner * per + at) * sources, 8), sources)
            right[place, :LANES] = (words >> 16).astype(jnp.float32)
            right[place, LANES:] = ((words << 16) >> 16).astype(jnp.float32)
    line = received[pl.ds(4, sources, stride=MESSAGE), :]
    lines = aligned(line, 0), aligned(line, 1)
    scales = []
    for pair in range(pair_count):
        octet, at = pair // 8, pair % 8 * looks
        scales.append(jnp.exp2(lines[0][at + 4 + octet : at + 5 + octet]) * (1.0 / 32767.0))
        total = lines[0][at + octet : at + octet + 1] + lines[1][at + 2 + octet : at + 3 + octet]
        left[pixels:, pair * sources : (pair + 1) * sources] = jnp.broadcast_to(
            total * scales[pair], (left.shape[0] - pixels, sources)
        )
    for half in range(2):
        for col in range(pixels // (2 * looks)):
            words = received[pl.ds(col * 2 + half, sources, stride=MESSAGE), :]
            for octet, value in enumerate((words >> 16, (words << 16) >> 16)):
                turned = aligned(value, half)
                for at in range(8):
                    pair = octet * 8 + at
                    row = (col * 2 + half) * looks
                    left[row : row + looks, pair * sources : (pair + 1) * sources] = (
                        turned[at * looks : (at + 1) * looks] * scales[pair]
                    )
    product = jnp.dot(
        left[...], right[...], precision=lax.Precision.HIGHEST, preferred_element_type=jnp.float32
    )
    out[...] = product[:pixels] * (1.0 / CODES)
    bias[...] = product[pixels:] * (1.0 / (CODES * band_pixels))


def invert(received, kept, swapped, pixels, band_pixels):
    total_pairs, dates = 2 * kept.shape[0], 2 * LANES
    vmem = pl.BlockSpec(memory_space=pltpu.VMEM)
    return pl.pallas_call(
        partial(invert_kernel, band_pixels),
        in_specs=[pl.BlockSpec(memory_space=pltpu.SMEM)] + [vmem] * 3,
        out_specs=[vmem] * 2,
        out_shape=[
            jax.ShapeDtypeStruct((pixels, dates), jnp.float32),
            jax.ShapeDtypeStruct((8, dates), jnp.float32),
        ],
        scratch_shapes=[
            pltpu.VMEM((pixels + 8, total_pairs), jnp.float32),
            pltpu.VMEM((total_pairs, dates), jnp.float32),
        ],
        compiler_params=pltpu.CompilerParams(vmem_limit_bytes=16 << 20),
        name="invert",
    )((lax.axis_index("date") % 2).reshape(1), received, kept, swapped)


def body(acquisitions, date_pairs, cycle_maps, inverse):
    group, _, height, width = acquisitions.shape
    devices = lax.axis_size("date")
    total_dates = group * devices
    pair_count, look_rows, look_cols = cycle_maps.shape
    rows = height // 2
    half = look_rows // 2

    def parts(images, start, stop):
        return images[:, :, :rows, start:stop], images[:, :, rows:, start:stop]

    def exchanged(pair):
        return passed_along(pair[0], "date", -1), passed_along(pair[1], "date", 1)

    low_pairs = passed_along(date_pairs, "date", 1)
    low_cycles = passed_along(cycle_maps, "date", 1)
    sent, left, low_pairs, low_cycles, date_pairs, inverse = lax.optimization_barrier(
        (parts(acquisitions, *CHUNKS[0]), acquisitions, low_pairs, low_cycles, date_pairs, inverse)
    )
    others = [exchanged(sent)]
    words, exponent = coded_inverse(inverse)
    line = exponent_line(exponent)
    for start, stop in CHUNKS[1:]:
        sent, left, words = lax.optimization_barrier((parts(left, start, stop), left, words))
        others.append(exchanged(sent))

    kept = sent_inverse(words)

    pairs = jnp.concatenate([date_pairs, low_pairs])
    gaps = (pairs[:, 1] - pairs[:, 0] + total_dates) % total_dates
    combos = pairs[:, 0] % group * group + gaps - 1
    late, words = lax.optimization_barrier((left, words))
    owned = [late[:, :, :, start:stop] for start, stop in CHUNKS]
    owned, combos = lax.optimization_barrier((owned, combos))
    looked = ()
    for (start, stop), own, (following, previous) in zip(CHUNKS, owned, others):
        final = stop == width
        rest = (combos, cycle_maps, low_cycles, line) if final else ()
        looked = (phases(start, stop, final, own, following, previous, looked, *rest),)

    payload, kept = lax.optimization_barrier((looked[0], kept))
    swapped = lax.ppermute(kept, "date", [(at, at ^ 1) for at in range(devices)])
    received = lax.all_to_all(
        payload.reshape(devices, 1, -1), "date", split_axis=0, concat_axis=0, tiled=True
    ).reshape(payload.shape)
    out_cols = look_cols // devices
    row_count = lax.axis_size("row")
    result, bias = invert(received, kept, swapped, out_cols * look_rows, look_rows * look_cols * row_count)
    for step in range(1, row_count):
        result = result - passed_along(bias, "row", step)[:1]
    result = result - bias[:1]
    return result.reshape(out_cols, look_rows, total_dates)


def solution(mesh):
    return jax.shard_map(
        body,
        mesh=mesh,
        in_specs=(
            P("date", None, "row", None),
            P("date", None),
            P("date", "row", None),
            P(None, "date"),
        ),
        out_specs=P("date", "row", None),
        check_vma=False,
    )
```

```python
from functools import partial
import math

import jax
import jax.numpy as jnp
from jax import lax
from jax.experimental import pallas as pl
from jax.experimental.pallas import tpu as pltpu
from jax.sharding import PartitionSpec as P

LOOK_R = 4
LOOK_C = 16
TWO_PI = 2.0 * math.pi
CODES = 32767.0 / TWO_PI
CHUNKS = ((0, 1536), (1536, 2048))
STEP = 512
MESSAGE = 5
LANES = 128
ATAN = (
    0.9999993329,
    -0.3332985605,
    0.1994653599,
    -0.1390853351,
    0.0964200441,
    -0.0559098861,
    0.0218612288,
    -0.0040540580,
)


def passed_along(value, axis, steps):
    count = lax.axis_size(axis)
    pairs = [(source, (source + steps) % count) for source in range(count)]
    return lax.ppermute(value, axis, pairs)


def arctan2(y, x):
    wide, tall = jnp.abs(x), jnp.abs(y)
    larger = jnp.maximum(wide, tall)
    ratio = jnp.minimum(wide, tall) / jnp.where(larger == 0.0, 1.0, larger)
    square = ratio * ratio
    value = jnp.full_like(square, ATAN[-1])
    for factor in ATAN[-2::-1]:
        value = value * square + factor
    value = value * ratio
    value = jnp.where(tall > wide, 0.5 * math.pi - value, value)
    value = jnp.where(x < 0.0, math.pi - value, value)
    return jnp.where(y < 0.0, -value, value)


def phase_kernel(first_col, last, final, own, following, previous, *refs):
    refs = list(refs)
    earlier = refs.pop(0) if first_col else None
    if final:
        combos, high_cycles, low_cycles, line, payload, images, high, low, picked, looked, cycles, sums, words = refs
    else:
        looked, images, high, low, picked = refs
    group, _, rows, _ = following.shape
    steps, width, _ = picked.shape
    looks = rows // LOOK_R
    pair_count = group * group
    step_cols = width // LOOK_C
    tiles = width // LANES
    for step in range(steps):
        shape = picked.shape[1:]
        of = lax.broadcasted_iota(jnp.int32, shape, 0) // LOOK_C + first_col + step * step_cols
        chosen = of == lax.broadcasted_iota(jnp.int32, shape, 1)
        picked[step] = jnp.where(chosen, 1.0, 0.0).astype(jnp.bfloat16)

    def widen(source, start, row, col):
        @pl.loop(0, 2 * group)
        def _(index):
            date, part = index // 2, index % 2
            for tile in range(tiles):
                lanes = pl.ds(pl.multiple_of(col + tile * LANES, LANES), LANES)
                images[start + date, part, tile] = source[date, part, pl.ds(row, rows), lanes].astype(jnp.float32)

    @pl.loop(0, 2 * steps)
    def _(index):
        half, step_at = index // steps, index % steps
        widen(own, half * group, pl.multiple_of(half * rows, rows), step_at * width)

        @pl.when(half == 0)
        def _():
            widen(following, group, 0, step_at * width)

        @pl.when(half == 1)
        def _():
            widen(previous, 0, 0, step_at * width)

        @pl.loop(0, tiles)
        def _(tile):
            lanes = pl.ds(pl.multiple_of(tile * LANES, LANES), LANES)
            for date in range(0, group, 2):
                totals = {}
                for block in range(looks // 8):
                    for step in range(LOOK_R):
                        at = pl.ds(block * 8 * LOOK_R + step, 8, stride=LOOK_R)
                        seen = {
                            image: [images[image, part, tile, at, :] for part in range(2)]
                            for image in range(date, date + group + 2)
                        }
                        for first in range(date, date + 2):
                            a0, a1 = seen[first]
                            for gap in range(group):
                                b0, b1 = seen[first + gap + 1]
                                re, im = a0 * b0 + a1 * b1, a1 * b0 - a0 * b1
                                for part, value in enumerate((re, im)):
                                    key = first, gap, part, block
                                    totals[key] = totals[key] + value if key in totals else value
                for first in range(date, date + 2):
                    for gap in range(group):
                        for part in range(2):
                            value = jnp.concatenate(
                                [totals[first, gap, part, block] for block in range(looks // 8)], axis=0
                            )
                            head = value.astype(jnp.bfloat16)
                            tail = (value - head.astype(jnp.float32)).astype(jnp.bfloat16)
                            start = (part * pair_count + first * group + gap) * looks
                            high[start : start + looks, lanes] = head
                            low[start : start + looks, lanes] = tail

        summed = jnp.dot(high[...], picked[step_at], preferred_element_type=jnp.float32)
        summed += jnp.dot(low[...], picked[step_at], preferred_element_type=jnp.float32)

        @pl.when(step_at == 0)
        def _():
            looked[half] = summed if earlier is None else earlier[half] + summed

        @pl.when(step_at > 0)
        def _():
            looked[half] += summed

    if not final:
        return
    cycles[0] = TWO_PI * high_cycles[:, :looks, :].astype(jnp.float32).reshape(cycles.shape[1:])
    cycles[1] = TWO_PI * low_cycles[:, looks:, :].astype(jnp.float32).reshape(cycles.shape[1:])

    @pl.loop(0, 2)
    def _(half):
        taken = []
        for part in range(2):
            for pair in range(pair_count):
                start = (part * pair_count + combos[half * pair_count + pair]) * looks
                taken.append(looked[half, pl.ds(pl.multiple_of(start, 8), looks), :])
        real = jnp.concatenate(taken[:pair_count], axis=0)
        imag = jnp.concatenate(taken[pair_count:], axis=0)
        codes = jnp.round((arctan2(imag, real) - cycles[half] + math.pi) * CODES).T
        total = jnp.sum(codes, axis=0, keepdims=True).astype(jnp.int32)
        codes = codes.astype(jnp.int32)
        for octet in range(2):
            sums[pl.ds(2 * half + octet, 1), :] = total[:, octet * LANES : (octet + 1) * LANES]
        words[...] = (codes[:, :LANES] << 16) | (codes[:, LANES:] & 0xFFFF)
        count = last // 2
        for col in range(2):
            payload[pl.ds(2 * col + half, count, stride=MESSAGE), :] = words[pl.ds(col, count, stride=2), :]

    total = sums[...]
    for step in (8, 4, 2, 1):
        total += pltpu.roll(total, LANES - step, 1)
    lane = lax.broadcasted_iota(jnp.int32, (1, LANES), 1) % looks
    full = line[0:1, :]
    for row in range(4):
        moved = pltpu.roll(total, row, 1)[row : row + 1]
        full = jnp.where(lane == row, moved, full)
    payload[pl.ds(4, last // 2, stride=MESSAGE), :] = jnp.broadcast_to(full, (last // 2, LANES))


def phases(start, stop, final, own, following, previous, earlier, *rest):
    group, _, height, _ = own.shape
    rows = height // 2
    looked_cols = LANES
    looks = rows // LOOK_R
    tiles = STEP // LANES
    pair_count = group * group
    steps = (stop - start) // STEP
    vmem = pl.BlockSpec(memory_space=pltpu.VMEM)
    in_specs = [vmem] * (3 + len(earlier))
    looked_shape = (2, 2 * pair_count * looks, looked_cols)
    out_shape = jax.ShapeDtypeStruct(looked_shape, jnp.float32)
    scratch = [
        pltpu.VMEM((2 * group, 2, tiles, rows, LANES), jnp.float32),
        pltpu.VMEM((2 * pair_count * looks, STEP), jnp.bfloat16),
        pltpu.VMEM((2 * pair_count * looks, STEP), jnp.bfloat16),
        pltpu.VMEM((steps, STEP, looked_cols), jnp.bfloat16),
    ]
    if final:
        in_specs += [pl.BlockSpec(memory_space=pltpu.SMEM)] + [vmem] * 3
        out_shape = jax.ShapeDtypeStruct((looked_cols // 2 * MESSAGE, LANES), jnp.int32)
        scratch += [
            pltpu.VMEM(looked_shape, jnp.float32),
            pltpu.VMEM((2, pair_count * looks, looked_cols), jnp.float32),
            pltpu.VMEM((8, LANES), jnp.int32),
            pltpu.VMEM((looked_cols, LANES), jnp.int32),
        ]
    return pl.pallas_call(
        partial(phase_kernel, start // LOOK_C, stop // LOOK_C, final),
        in_specs=in_specs,
        out_specs=vmem,
        out_shape=out_shape,
        scratch_shapes=scratch,
        compiler_params=pltpu.CompilerParams(vmem_limit_bytes=16 << 20),
        cost_estimate=pl.CostEstimate(
            flops=8 * pair_count * height * (stop - start),
            bytes_accessed=group * 4 * height * (stop - start) * 2,
            transcendentals=0,
        ),
        name="phases",
    )(own, following, previous, *earlier, *rest)


def coded_inverse(inverse):
    turned = inverse.T
    peak = jnp.max(jnp.abs(turned), axis=1, keepdims=True)
    exponent = jnp.clip(jnp.floor(jnp.log2(peak)) + 1.0, -100.0, 100.0)
    codes = jnp.round(turned * jnp.exp2(-exponent) * 32767.0).astype(jnp.int32)
    words = (codes[:, :LANES] << 16) | (codes[:, LANES:] & 0xFFFF)
    return words, exponent[:, 0].astype(jnp.int32)


def exponent_line(exponent):
    spread = exponent.reshape(2, -1).T
    spread = jnp.pad(spread, ((0, 0), (4, LANES // spread.shape[0] - 6)))
    return jnp.broadcast_to(spread.reshape(1, LANES), (8, LANES))


def sent_inverse(words):
    devices = lax.axis_size("date")
    per = words.shape[0] // 2
    sent = jnp.broadcast_to(words.reshape(1, 2, per, LANES), (devices // 2, 2, per, LANES))
    got = lax.all_to_all(
        sent.reshape(devices, per, LANES), "date", split_axis=0, concat_axis=0, tiled=True
    ).reshape(-1, LANES)
    return got


def invert_kernel(band_pixels, side, received, kept, swapped, out, bias, left, right):
    pair_count = 16
    per = pair_count // 2
    sources = kept.shape[0] // per
    looks = LANES * 2 // pair_count
    pixels = out.shape[0]

    def aligned(words, half):
        value = words.astype(jnp.float32)
        return (pltpu.roll(value, sources - 1, 0) if half else value).T

    for at in range(per):
        for owner, source in ((side[0], kept), (1 - side[0], swapped)):
            words = source[pl.ds(at, sources, stride=per), :]
            place = pl.ds(pl.multiple_of((owner * per + at) * sources, 8), sources)
            right[place, :LANES] = (words >> 16).astype(jnp.float32)
            right[place, LANES:] = ((words << 16) >> 16).astype(jnp.float32)
    line = received[pl.ds(4, sources, stride=MESSAGE), :]
    lines = aligned(line, 0), aligned(line, 1)
    scales = []
    for pair in range(pair_count):
        octet, at = pair // 8, pair % 8 * looks
        scales.append(jnp.exp2(lines[0][at + 4 + octet : at + 5 + octet]) * (1.0 / 32767.0))
        total = lines[0][at + octet : at + octet + 1] + lines[1][at + 2 + octet : at + 3 + octet]
        left[pixels:, pair * sources : (pair + 1) * sources] = jnp.broadcast_to(
            total * scales[pair], (left.shape[0] - pixels, sources)
        )
    for half in range(2):
        for col in range(pixels // (2 * looks)):
            words = received[pl.ds(col * 2 + half, sources, stride=MESSAGE), :]
            for octet, value in enumerate((words >> 16, (words << 16) >> 16)):
                turned = aligned(value, half)
                for at in range(8):
                    pair = octet * 8 + at
                    row = (col * 2 + half) * looks
                    left[row : row + looks, pair * sources : (pair + 1) * sources] = (
                        turned[at * looks : (at + 1) * looks] * scales[pair]
                    )
    product = jnp.dot(
        left[...], right[...], precision=lax.Precision.HIGHEST, preferred_element_type=jnp.float32
    )
    out[...] = product[:pixels] * (1.0 / CODES)
    bias[...] = product[pixels:] * (1.0 / (CODES * band_pixels))


def invert(received, kept, swapped, pixels, band_pixels):
    total_pairs, dates = 2 * kept.shape[0], 2 * LANES
    vmem = pl.BlockSpec(memory_space=pltpu.VMEM)
    return pl.pallas_call(
        partial(invert_kernel, band_pixels),
        in_specs=[pl.BlockSpec(memory_space=pltpu.SMEM)] + [vmem] * 3,
        out_specs=[vmem] * 2,
        out_shape=[
            jax.ShapeDtypeStruct((pixels, dates), jnp.float32),
            jax.ShapeDtypeStruct((8, dates), jnp.float32),
        ],
        scratch_shapes=[
            pltpu.VMEM((pixels + 8, total_pairs), jnp.float32),
            pltpu.VMEM((total_pairs, dates), jnp.float32),
        ],
        compiler_params=pltpu.CompilerParams(vmem_limit_bytes=16 << 20),
        name="invert",
    )((lax.axis_index("date") % 2).reshape(1), received, kept, swapped)


def body(acquisitions, date_pairs, cycle_maps, inverse):
    group, _, height, width = acquisitions.shape
    devices = lax.axis_size("date")
    total_dates = group * devices
    pair_count, look_rows, look_cols = cycle_maps.shape
    rows = height // 2
    half = look_rows // 2

    def parts(images, start, stop):
        return images[:, :, :rows, start:stop], images[:, :, rows:, start:stop]

    def exchanged(pair):
        return passed_along(pair[0], "date", -1), passed_along(pair[1], "date", 1)

    low_pairs = passed_along(date_pairs, "date", 1)
    low_cycles = passed_along(cycle_maps, "date", 1)
    sent, left, low_pairs, low_cycles, date_pairs, inverse = lax.optimization_barrier(
        (parts(acquisitions, *CHUNKS[0]), acquisitions, low_pairs, low_cycles, date_pairs, inverse)
    )
    others = [exchanged(sent)]
    words, exponent = coded_inverse(inverse)
    line = exponent_line(exponent)
    for start, stop in CHUNKS[1:]:
        sent, left, words = lax.optimization_barrier((parts(left, start, stop), left, words))
        others.append(exchanged(sent))

    kept = sent_inverse(words)

    pairs = jnp.concatenate([date_pairs, low_pairs])
    gaps = (pairs[:, 1] - pairs[:, 0] + total_dates) % total_dates
    combos = pairs[:, 0] % group * group + gaps - 1
    late, words = lax.optimization_barrier((left, words))
    owned = [late[:, :, :, start:stop] for start, stop in CHUNKS]
    owned, combos = lax.optimization_barrier((owned, combos))
    looked = ()
    for (start, stop), own, (following, previous) in zip(CHUNKS, owned, others):
        final = stop == width
        rest = (combos, cycle_maps, low_cycles, line) if final else ()
        looked = (phases(start, stop, final, own, following, previous, looked, *rest),)

    payload, kept = lax.optimization_barrier((looked[0], kept))
    swapped = lax.ppermute(kept, "date", [(at, at ^ 1) for at in range(devices)])
    received = lax.all_to_all(
        payload.reshape(devices, 1, -1), "date", split_axis=0, concat_axis=0, tiled=True
    ).reshape(payload.shape)
    out_cols = look_cols // devices
    row_count = lax.axis_size("row")
    result, bias = invert(received, kept, swapped, out_cols * look_rows, look_rows * look_cols * row_count)
    for step in range(1, row_count):
        result = result - passed_along(bias, "row", step)[:1]
    result = result - bias[:1]
    return result.reshape(out_cols, look_rows, total_dates)


def solution(mesh):
    return jax.shard_map(
        body,
        mesh=mesh,
        in_specs=(
            P("date", None, "row", None),
            P("date", None),
            P("date", "row", None),
            P(None, "date"),
        ),
        out_specs=P("date", "row", None),
        check_vma=False,
    )
```

```python
from functools import partial
import math

import jax
import jax.numpy as jnp
from jax import lax
from jax.experimental import pallas as pl
from jax.experimental.pallas import tpu as pltpu
from jax.sharding import PartitionSpec as P

LOOK_R = 4
LOOK_C = 16
TWO_PI = 2.0 * math.pi
CODES = 32767.0 / TWO_PI
CHUNKS = ((0, 1536), (1536, 2048))
STEP = 512
MESSAGE = 5
LANES = 128
ATAN = (
    0.9999993329,
    -0.3332985605,
    0.1994653599,
    -0.1390853351,
    0.0964200441,
    -0.0559098861,
    0.0218612288,
    -0.0040540580,
)


def passed_along(value, axis, steps):
    count = lax.axis_size(axis)
    pairs = [(source, (source + steps) % count) for source in range(count)]
    return lax.ppermute(value, axis, pairs)


def arctan2(y, x):
    wide, tall = jnp.abs(x), jnp.abs(y)
    larger = jnp.maximum(wide, tall)
    ratio = jnp.minimum(wide, tall) / jnp.where(larger == 0.0, 1.0, larger)
    square = ratio * ratio
    value = jnp.full_like(square, ATAN[-1])
    for factor in ATAN[-2::-1]:
        value = value * square + factor
    value = value * ratio
    value = jnp.where(tall > wide, 0.5 * math.pi - value, value)
    value = jnp.where(x < 0.0, math.pi - value, value)
    return jnp.where(y < 0.0, -value, value)


def phase_kernel(first_col, last, sides, final, own, *refs):
    refs = list(refs)
    others = [refs.pop(0) for _ in sides]
    earlier = [refs.pop(0) for _ in sides] if first_col else None
    if final:
        combos, high_cycles, low_cycles, line, payload, held, arrived, images, high, low, picked = refs[:11]
        looked, cycles, sums, words = refs[11:]
    else:
        looked, held, arrived, images, high, low, picked = refs
    group, _, rows, _ = others[0].shape
    steps, width, _ = picked.shape
    looks = rows // LOOK_R
    pair_count = group * group
    step_cols = width // LOOK_C
    tiles = width // LANES
    copies = [
        pltpu.make_async_copy(
            other.at[:, :, :, pl.ds(step * width, width)],
            held.at[at * steps + step],
            arrived.at[at * steps + step],
        )
        for at, other in enumerate(others)
        for step in range(steps)
    ]
    for copy in copies:
        copy.start()
    for step in range(steps):
        shape = picked.shape[1:]
        of = lax.broadcasted_iota(jnp.int32, shape, 0) // LOOK_C + first_col + step * step_cols
        chosen = of == lax.broadcasted_iota(jnp.int32, shape, 1)
        picked[step] = jnp.where(chosen, 1.0, 0.0).astype(jnp.bfloat16)

    def widen(source, start, row, col):
        @pl.loop(0, 2 * group)
        def _(index):
            date, part = index // 2, index % 2
            for tile in range(tiles):
                lanes = pl.ds(pl.multiple_of(col + tile * LANES, LANES), LANES)
                images[start + date, part, tile] = source[date, part, pl.ds(row, rows), lanes].astype(jnp.float32)

    @pl.loop(0, len(sides) * steps)
    def _(index):
        at, step_at = index // steps, index % steps
        half = at + sides[0]
        widen(own, half * group, pl.multiple_of(half * rows, rows), step_at * width)
        for piece, copy in enumerate(copies):
            pl.when(index == piece)(copy.wait)
        widen(held.at[index], (1 - half) * group, 0, 0)

        @pl.loop(0, tiles)
        def _(tile):
            lanes = pl.ds(pl.multiple_of(tile * LANES, LANES), LANES)
            for date in range(0, group, 2):
                totals = {}
                for block in range(looks // 8):
                    for step in range(LOOK_R):
                        lines = pl.ds(block * 8 * LOOK_R + step, 8, stride=LOOK_R)
                        seen = {
                            image: [images[image, part, tile, lines, :] for part in range(2)]
                            for image in range(date, date + group + 2)
                        }
                        for first in range(date, date + 2):
                            a0, a1 = seen[first]
                            for gap in range(group):
                                b0, b1 = seen[first + gap + 1]
                                re, im = a0 * b0 + a1 * b1, a1 * b0 - a0 * b1
                                for part, value in enumerate((re, im)):
                                    key = first, gap, part, block
                                    totals[key] = totals[key] + value if key in totals else value
                for first in range(date, date + 2):
                    for gap in range(group):
                        for part in range(2):
                            value = jnp.concatenate(
                                [totals[first, gap, part, block] for block in range(looks // 8)], axis=0
                            )
                            head = value.astype(jnp.bfloat16)
                            tail = (value - head.astype(jnp.float32)).astype(jnp.bfloat16)
                            start = (part * pair_count + first * group + gap) * looks
                            high[start : start + looks, lanes] = head
                            low[start : start + looks, lanes] = tail

        summed = jnp.dot(high[...], picked[step_at], preferred_element_type=jnp.float32)
        summed += jnp.dot(low[...], picked[step_at], preferred_element_type=jnp.float32)

        for place in range(len(sides)):

            @pl.when(index == place * steps)
            def _(place=place):
                looked[place] = summed if earlier is None else earlier[place][0] + summed

        @pl.when(step_at > 0)
        def _():
            looked[at] += summed

    if not final:
        return
    cycles[0] = TWO_PI * high_cycles[:, :looks, :].astype(jnp.float32).reshape(cycles.shape[1:])
    cycles[1] = TWO_PI * low_cycles[:, looks:, :].astype(jnp.float32).reshape(cycles.shape[1:])

    @pl.loop(0, 2)
    def _(half):
        taken = []
        for part in range(2):
            for pair in range(pair_count):
                start = (part * pair_count + combos[half * pair_count + pair]) * looks
                taken.append(looked[half, pl.ds(pl.multiple_of(start, 8), looks), :])
        real = jnp.concatenate(taken[:pair_count], axis=0)
        imag = jnp.concatenate(taken[pair_count:], axis=0)
        codes = jnp.round((arctan2(imag, real) - cycles[half] + math.pi) * CODES).T
        total = jnp.sum(codes, axis=0, keepdims=True).astype(jnp.int32)
        codes = codes.astype(jnp.int32)
        for octet in range(2):
            sums[pl.ds(2 * half + octet, 1), :] = total[:, octet * LANES : (octet + 1) * LANES]
        words[...] = (codes[:, :LANES] << 16) | (codes[:, LANES:] & 0xFFFF)
        count = last // 2
        for col in range(2):
            payload[pl.ds(2 * col + half, count, stride=MESSAGE), :] = words[pl.ds(col, count, stride=2), :]

    total = sums[...]
    for step in (8, 4, 2, 1):
        total += pltpu.roll(total, LANES - step, 1)
    lane = lax.broadcasted_iota(jnp.int32, (1, LANES), 1) % looks
    full = line[0:1, :]
    for row in range(4):
        moved = pltpu.roll(total, row, 1)[row : row + 1]
        full = jnp.where(lane == row, moved, full)
    payload[pl.ds(4, last // 2, stride=MESSAGE), :] = jnp.broadcast_to(full, (last // 2, LANES))


def phases(start, stop, sides, final, own, others, earlier, *rest):
    group, _, height, _ = own.shape
    rows = height // 2
    looked_cols = LANES
    looks = rows // LOOK_R
    tiles = STEP // LANES
    pair_count = group * group
    steps = (stop - start) // STEP
    vmem = pl.BlockSpec(memory_space=pltpu.VMEM)
    in_specs = [vmem] + [pl.BlockSpec(memory_space=pl.ANY)] * len(others) + [vmem] * len(earlier)
    looked_shape = (len(sides), 2 * pair_count * looks, looked_cols)
    out_shape = jax.ShapeDtypeStruct(looked_shape, jnp.float32)
    scratch = [
        pltpu.VMEM((len(sides) * steps, group, 2, rows, STEP), jnp.bfloat16),
        pltpu.SemaphoreType.DMA((len(sides) * steps,)),
        pltpu.VMEM((2 * group, 2, tiles, rows, LANES), jnp.float32),
        pltpu.VMEM((2 * pair_count * looks, STEP), jnp.bfloat16),
        pltpu.VMEM((2 * pair_count * looks, STEP), jnp.bfloat16),
        pltpu.VMEM((steps, STEP, looked_cols), jnp.bfloat16),
    ]
    if final:
        in_specs += [pl.BlockSpec(memory_space=pltpu.SMEM)] + [vmem] * 3
        out_shape = jax.ShapeDtypeStruct((looked_cols // 2 * MESSAGE, LANES), jnp.int32)
        scratch += [
            pltpu.VMEM(looked_shape, jnp.float32),
            pltpu.VMEM((2, pair_count * looks, looked_cols), jnp.float32),
            pltpu.VMEM((8, LANES), jnp.int32),
            pltpu.VMEM((looked_cols, LANES), jnp.int32),
        ]
    return pl.pallas_call(
        partial(phase_kernel, start // LOOK_C, stop // LOOK_C, sides, final),
        in_specs=in_specs,
        out_specs=vmem,
        out_shape=out_shape,
        scratch_shapes=scratch,
        compiler_params=pltpu.CompilerParams(vmem_limit_bytes=16 << 20),
        cost_estimate=pl.CostEstimate(
            flops=8 * pair_count * rows * len(sides) * (stop - start),
            bytes_accessed=group * 4 * height * (stop - start) * 2,
            transcendentals=0,
        ),
        name="phases",
    )(own, *others, *earlier, *rest)


def coded_inverse(inverse):
    turned = inverse.T
    peak = jnp.max(jnp.abs(turned), axis=1, keepdims=True)
    exponent = jnp.clip(jnp.floor(jnp.log2(peak)) + 1.0, -100.0, 100.0)
    codes = jnp.round(turned * jnp.exp2(-exponent) * 32767.0).astype(jnp.int32)
    words = (codes[:, :LANES] << 16) | (codes[:, LANES:] & 0xFFFF)
    return words, exponent[:, 0].astype(jnp.int32)


def exponent_line(exponent):
    spread = exponent.reshape(2, -1).T
    spread = jnp.pad(spread, ((0, 0), (4, LANES // spread.shape[0] - 6)))
    return jnp.broadcast_to(spread.reshape(1, LANES), (8, LANES))


def sent_inverse(words):
    devices = lax.axis_size("date")
    per = words.shape[0] // 2
    sent = jnp.broadcast_to(words.reshape(1, 2, per, LANES), (devices // 2, 2, per, LANES))
    got = lax.all_to_all(
        sent.reshape(devices, per, LANES), "date", split_axis=0, concat_axis=0, tiled=True
    ).reshape(-1, LANES)
    return got


def invert_kernel(band_pixels, side, received, kept, swapped, out, bias, left, right):
    pair_count = 16
    per = pair_count // 2
    sources = kept.shape[0] // per
    looks = LANES * 2 // pair_count
    pixels = out.shape[0]

    def aligned(words, half):
        value = words.astype(jnp.float32)
        return (pltpu.roll(value, sources - 1, 0) if half else value).T

    for at in range(per):
        for owner, source in ((side[0], kept), (1 - side[0], swapped)):
            words = source[pl.ds(at, sources, stride=per), :]
            place = pl.ds(pl.multiple_of((owner * per + at) * sources, 8), sources)
            right[place, :LANES] = (words >> 16).astype(jnp.float32)
            right[place, LANES:] = ((words << 16) >> 16).astype(jnp.float32)
    line = received[pl.ds(4, sources, stride=MESSAGE), :]
    lines = aligned(line, 0), aligned(line, 1)
    scales = []
    for pair in range(pair_count):
        octet, at = pair // 8, pair % 8 * looks
        scales.append(jnp.exp2(lines[0][at + 4 + octet : at + 5 + octet]) * (1.0 / 32767.0))
        total = lines[0][at + octet : at + octet + 1] + lines[1][at + 2 + octet : at + 3 + octet]
        left[pixels:, pair * sources : (pair + 1) * sources] = jnp.broadcast_to(
            total * scales[pair], (left.shape[0] - pixels, sources)
        )
    for half in range(2):
        for col in range(pixels // (2 * looks)):
            words = received[pl.ds(col * 2 + half, sources, stride=MESSAGE), :]
            for octet, value in enumerate((words >> 16, (words << 16) >> 16)):
                turned = aligned(value, half)
                for at in range(8):
                    pair = octet * 8 + at
                    row = (col * 2 + half) * looks
                    left[row : row + looks, pair * sources : (pair + 1) * sources] = (
                        turned[at * looks : (at + 1) * looks] * scales[pair]
                    )
    product = jnp.dot(
        left[...], right[...], precision=lax.Precision.HIGHEST, preferred_element_type=jnp.float32
    )
    out[...] = product[:pixels] * (1.0 / CODES)
    bias[...] = product[pixels:] * (1.0 / (CODES * band_pixels))


def invert(received, kept, swapped, pixels, band_pixels):
    total_pairs, dates = 2 * kept.shape[0], 2 * LANES
    vmem = pl.BlockSpec(memory_space=pltpu.VMEM)
    return pl.pallas_call(
        partial(invert_kernel, band_pixels),
        in_specs=[pl.BlockSpec(memory_space=pltpu.SMEM)] + [vmem] * 3,
        out_specs=[vmem] * 2,
        out_shape=[
            jax.ShapeDtypeStruct((pixels, dates), jnp.float32),
            jax.ShapeDtypeStruct((8, dates), jnp.float32),
        ],
        scratch_shapes=[
            pltpu.VMEM((pixels + 8, total_pairs), jnp.float32),
            pltpu.VMEM((total_pairs, dates), jnp.float32),
        ],
        compiler_params=pltpu.CompilerParams(vmem_limit_bytes=16 << 20),
        name="invert",
    )((lax.axis_index("date") % 2).reshape(1), received, kept, swapped)


def body(acquisitions, date_pairs, cycle_maps, inverse):
    group, _, height, width = acquisitions.shape
    devices = lax.axis_size("date")
    total_dates = group * devices
    pair_count, look_rows, look_cols = cycle_maps.shape
    rows = height // 2
    half = look_rows // 2

    def parts(images, start, stop):
        return images[:, :, :rows, start:stop], images[:, :, rows:, start:stop]

    def exchanged(pair):
        return passed_along(pair[0], "date", -1), passed_along(pair[1], "date", 1)

    low_pairs = passed_along(date_pairs, "date", 1)
    low_cycles = passed_along(cycle_maps, "date", 1)
    sent, left, low_pairs, low_cycles, date_pairs, inverse = lax.optimization_barrier(
        (parts(acquisitions, *CHUNKS[0]), acquisitions, low_pairs, low_cycles, date_pairs, inverse)
    )
    others = [exchanged(sent)]
    words, exponent = coded_inverse(inverse)
    line = exponent_line(exponent)
    for start, stop in CHUNKS[1:]:
        sent, left, words = lax.optimization_barrier((parts(left, start, stop), left, words))
        others.append(exchanged(sent))

    kept = sent_inverse(words)

    pairs = jnp.concatenate([date_pairs, low_pairs])
    gaps = (pairs[:, 1] - pairs[:, 0] + total_dates) % total_dates
    combos = pairs[:, 0] % group * group + gaps - 1
    late, words = lax.optimization_barrier((left, words))
    owned = [late[:, :, :, start:stop] for start, stop in CHUNKS]
    owned, combos = lax.optimization_barrier((owned, combos))
    looked = ()
    for (start, stop), own, received in zip(CHUNKS, owned, others):
        if stop < width:
            upper = phases(start, stop, (0,), False, own, received[:1], looked[:1])
            lower, upper = lax.optimization_barrier((received[1:], upper))
            looked = [upper, phases(start, stop, (1,), False, own, lower, looked[1:])]
        else:
            payload = phases(
                start, stop, (0, 1), True, own, received, looked, combos, cycle_maps, low_cycles, line
            )

    payload, kept = lax.optimization_barrier((payload, kept))
    swapped = lax.ppermute(kept, "date", [(at, at ^ 1) for at in range(devices)])
    received = lax.all_to_all(
        payload.reshape(devices, 1, -1), "date", split_axis=0, concat_axis=0, tiled=True
    ).reshape(payload.shape)
    out_cols = look_cols // devices
    row_count = lax.axis_size("row")
    result, bias = invert(received, kept, swapped, out_cols * look_rows, look_rows * look_cols * row_count)
    for step in range(1, row_count):
        result = result - passed_along(bias, "row", step)[:1]
    result = result - bias[:1]
    return result.reshape(out_cols, look_rows, total_dates)


def solution(mesh):
    return jax.shard_map(
        body,
        mesh=mesh,
        in_specs=(
            P("date", None, "row", None),
            P("date", None),
            P("date", "row", None),
            P(None, "date"),
        ),
        out_specs=P("date", "row", None),
        check_vma=False,
    )
```

```python
from functools import partial
import math

import jax
import jax.numpy as jnp
from jax import lax
from jax.experimental import pallas as pl
from jax.experimental.pallas import tpu as pltpu
from jax.sharding import PartitionSpec as P

LOOK_R = 4
LOOK_C = 16
TWO_PI = 2.0 * math.pi
CODES = 32767.0 / TWO_PI
CHUNKS = ((0, 1536), (1536, 2048))
STEP = 512
MESSAGE = 5
LANES = 128
ATAN = (
    0.9999993329,
    -0.3332985605,
    0.1994653599,
    -0.1390853351,
    0.0964200441,
    -0.0559098861,
    0.0218612288,
    -0.0040540580,
)


def passed_along(value, axis, steps):
    count = lax.axis_size(axis)
    pairs = [(source, (source + steps) % count) for source in range(count)]
    return lax.ppermute(value, axis, pairs)


def arctan2(y, x):
    wide, tall = jnp.abs(x), jnp.abs(y)
    larger = jnp.maximum(wide, tall)
    ratio = jnp.minimum(wide, tall) / jnp.where(larger == 0.0, 1.0, larger)
    square = ratio * ratio
    value = jnp.full_like(square, ATAN[-1])
    for factor in ATAN[-2::-1]:
        value = value * square + factor
    value = value * ratio
    value = jnp.where(tall > wide, 0.5 * math.pi - value, value)
    value = jnp.where(x < 0.0, math.pi - value, value)
    return jnp.where(y < 0.0, -value, value)


def phase_kernel(first_col, last, sides, final, own, *refs):
    refs = list(refs)
    others = [refs.pop(0) for _ in sides]
    earlier = [refs.pop(0) for _ in sides] if first_col else None
    if final:
        finished = refs.pop(0)
        combos, high_cycles, low_cycles, line, payload, held, arrived, images, high, low, picked = refs[:11]
        looked, cycles, sums, words = refs[11:]
    else:
        looked, held, arrived, images, high, low, picked = refs
    group, _, rows, _ = others[0].shape
    steps, width, _ = picked.shape
    looks = rows // LOOK_R
    pair_count = group * group
    step_cols = width // LOOK_C
    tiles = width // LANES
    copies = [
        pltpu.make_async_copy(
            other.at[:, :, :, pl.ds(step * width, width)],
            held.at[at * steps + step],
            arrived.at[at * steps + step],
        )
        for at, other in enumerate(others)
        for step in range(steps)
    ]
    for copy in copies:
        copy.start()
    shift = sides[0] if final else 0
    if final:
        looked[0] = finished[0]
    for step in range(steps):
        shape = picked.shape[1:]
        of = lax.broadcasted_iota(jnp.int32, shape, 0) // LOOK_C + first_col + step * step_cols
        chosen = of == lax.broadcasted_iota(jnp.int32, shape, 1)
        picked[step] = jnp.where(chosen, 1.0, 0.0).astype(jnp.bfloat16)

    def widen(source, start, row, col):
        @pl.loop(0, 2 * group)
        def _(index):
            date, part = index // 2, index % 2
            for tile in range(tiles):
                lanes = pl.ds(pl.multiple_of(col + tile * LANES, LANES), LANES)
                images[start + date, part, tile] = source[date, part, pl.ds(row, rows), lanes].astype(jnp.float32)

    @pl.loop(0, len(sides) * steps)
    def _(index):
        at, step_at = index // steps, index % steps
        half = at + sides[0]
        widen(own, half * group, pl.multiple_of(half * rows, rows), step_at * width)
        for piece, copy in enumerate(copies):
            pl.when(index == piece)(copy.wait)
        widen(held.at[index], (1 - half) * group, 0, 0)

        @pl.loop(0, tiles)
        def _(tile):
            lanes = pl.ds(pl.multiple_of(tile * LANES, LANES), LANES)
            for date in range(0, group, 2):
                totals = {}
                for block in range(looks // 8):
                    for step in range(LOOK_R):
                        lines = pl.ds(block * 8 * LOOK_R + step, 8, stride=LOOK_R)
                        seen = {
                            image: [images[image, part, tile, lines, :] for part in range(2)]
                            for image in range(date, date + group + 2)
                        }
                        for first in range(date, date + 2):
                            a0, a1 = seen[first]
                            for gap in range(group):
                                b0, b1 = seen[first + gap + 1]
                                re, im = a0 * b0 + a1 * b1, a1 * b0 - a0 * b1
                                for part, value in enumerate((re, im)):
                                    key = first, gap, part, block
                                    totals[key] = totals[key] + value if key in totals else value
                for first in range(date, date + 2):
                    for gap in range(group):
                        for part in range(2):
                            value = jnp.concatenate(
                                [totals[first, gap, part, block] for block in range(looks // 8)], axis=0
                            )
                            head = value.astype(jnp.bfloat16)
                            tail = (value - head.astype(jnp.float32)).astype(jnp.bfloat16)
                            start = (part * pair_count + first * group + gap) * looks
                            high[start : start + looks, lanes] = head
                            low[start : start + looks, lanes] = tail

        summed = jnp.dot(high[...], picked[step_at], preferred_element_type=jnp.float32)
        summed += jnp.dot(low[...], picked[step_at], preferred_element_type=jnp.float32)

        for place in range(len(sides)):

            @pl.when(index == place * steps)
            def _(place=place):
                looked[place + shift] = summed if earlier is None else earlier[place][0] + summed

        @pl.when(step_at > 0)
        def _():
            looked[at + shift] += summed

    if not final:
        return
    cycles[0] = TWO_PI * high_cycles[:, :looks, :].astype(jnp.float32).reshape(cycles.shape[1:])
    cycles[1] = TWO_PI * low_cycles[:, looks:, :].astype(jnp.float32).reshape(cycles.shape[1:])

    @pl.loop(0, 2)
    def _(half):
        taken = []
        for part in range(2):
            for pair in range(pair_count):
                start = (part * pair_count + combos[half * pair_count + pair]) * looks
                taken.append(looked[half, pl.ds(pl.multiple_of(start, 8), looks), :])
        real = jnp.concatenate(taken[:pair_count], axis=0)
        imag = jnp.concatenate(taken[pair_count:], axis=0)
        codes = jnp.round((arctan2(imag, real) - cycles[half] + math.pi) * CODES).T
        total = jnp.sum(codes, axis=0, keepdims=True).astype(jnp.int32)
        codes = codes.astype(jnp.int32)
        for octet in range(2):
            sums[pl.ds(2 * half + octet, 1), :] = total[:, octet * LANES : (octet + 1) * LANES]
        words[...] = (codes[:, :LANES] << 16) | (codes[:, LANES:] & 0xFFFF)
        count = last // 2
        for col in range(2):
            payload[pl.ds(2 * col + half, count, stride=MESSAGE), :] = words[pl.ds(col, count, stride=2), :]

    total = sums[...]
    for step in (8, 4, 2, 1):
        total += pltpu.roll(total, LANES - step, 1)
    lane = lax.broadcasted_iota(jnp.int32, (1, LANES), 1) % looks
    full = line[0:1, :]
    for row in range(4):
        moved = pltpu.roll(total, row, 1)[row : row + 1]
        full = jnp.where(lane == row, moved, full)
    payload[pl.ds(4, last // 2, stride=MESSAGE), :] = jnp.broadcast_to(full, (last // 2, LANES))


def phases(start, stop, sides, final, own, others, earlier, *rest):
    group, _, height, _ = own.shape
    rows = height // 2
    looked_cols = LANES
    looks = rows // LOOK_R
    tiles = STEP // LANES
    pair_count = group * group
    steps = (stop - start) // STEP
    vmem = pl.BlockSpec(memory_space=pltpu.VMEM)
    in_specs = [vmem] + [pl.BlockSpec(memory_space=pl.ANY)] * len(others) + [vmem] * len(earlier)
    looked_shape = (len(sides), 2 * pair_count * looks, looked_cols)
    out_shape = jax.ShapeDtypeStruct(looked_shape, jnp.float32)
    scratch = [
        pltpu.VMEM((len(sides) * steps, group, 2, rows, STEP), jnp.bfloat16),
        pltpu.SemaphoreType.DMA((len(sides) * steps,)),
        pltpu.VMEM((2 * group, 2, tiles, rows, LANES), jnp.float32),
        pltpu.VMEM((2 * pair_count * looks, STEP), jnp.bfloat16),
        pltpu.VMEM((2 * pair_count * looks, STEP), jnp.bfloat16),
        pltpu.VMEM((steps, STEP, looked_cols), jnp.bfloat16),
    ]
    if final:
        in_specs += [vmem, pl.BlockSpec(memory_space=pltpu.SMEM)] + [vmem] * 3
        out_shape = jax.ShapeDtypeStruct((looked_cols // 2 * MESSAGE, LANES), jnp.int32)
        scratch += [
            pltpu.VMEM((2, 2 * pair_count * looks, looked_cols), jnp.float32),
            pltpu.VMEM((2, pair_count * looks, looked_cols), jnp.float32),
            pltpu.VMEM((8, LANES), jnp.int32),
            pltpu.VMEM((looked_cols, LANES), jnp.int32),
        ]
    return pl.pallas_call(
        partial(phase_kernel, start // LOOK_C, stop // LOOK_C, sides, final),
        in_specs=in_specs,
        out_specs=vmem,
        out_shape=out_shape,
        scratch_shapes=scratch,
        compiler_params=pltpu.CompilerParams(vmem_limit_bytes=16 << 20),
        cost_estimate=pl.CostEstimate(
            flops=8 * pair_count * rows * len(sides) * (stop - start),
            bytes_accessed=group * 4 * height * (stop - start) * 2,
            transcendentals=0,
        ),
        name="phases",
    )(own, *others, *earlier, *rest)


def coded_inverse(inverse):
    turned = inverse.T
    peak = jnp.max(jnp.abs(turned), axis=1, keepdims=True)
    exponent = jnp.clip(jnp.floor(jnp.log2(peak)) + 1.0, -100.0, 100.0)
    codes = jnp.round(turned * jnp.exp2(-exponent) * 32767.0).astype(jnp.int32)
    words = (codes[:, :LANES] << 16) | (codes[:, LANES:] & 0xFFFF)
    return words, exponent[:, 0].astype(jnp.int32)


def exponent_line(exponent):
    spread = exponent.reshape(2, -1).T
    spread = jnp.pad(spread, ((0, 0), (4, LANES // spread.shape[0] - 6)))
    return jnp.broadcast_to(spread.reshape(1, LANES), (8, LANES))


def sent_inverse(words):
    devices = lax.axis_size("date")
    per = words.shape[0] // 2
    sent = jnp.broadcast_to(words.reshape(1, 2, per, LANES), (devices // 2, 2, per, LANES))
    got = lax.all_to_all(
        sent.reshape(devices, per, LANES), "date", split_axis=0, concat_axis=0, tiled=True
    ).reshape(-1, LANES)
    return got


def invert_kernel(band_pixels, side, received, kept, swapped, out, bias, left, right):
    pair_count = 16
    per = pair_count // 2
    sources = kept.shape[0] // per
    looks = LANES * 2 // pair_count
    pixels = out.shape[0]

    def aligned(words, half):
        value = words.astype(jnp.float32)
        return (pltpu.roll(value, sources - 1, 0) if half else value).T

    for at in range(per):
        for owner, source in ((side[0], kept), (1 - side[0], swapped)):
            words = source[pl.ds(at, sources, stride=per), :]
            place = pl.ds(pl.multiple_of((owner * per + at) * sources, 8), sources)
            right[place, :LANES] = (words >> 16).astype(jnp.float32)
            right[place, LANES:] = ((words << 16) >> 16).astype(jnp.float32)
    line = received[pl.ds(4, sources, stride=MESSAGE), :]
    lines = aligned(line, 0), aligned(line, 1)
    scales = []
    for pair in range(pair_count):
        octet, at = pair // 8, pair % 8 * looks
        scales.append(jnp.exp2(lines[0][at + 4 + octet : at + 5 + octet]) * (1.0 / 32767.0))
        total = lines[0][at + octet : at + octet + 1] + lines[1][at + 2 + octet : at + 3 + octet]
        left[pixels:, pair * sources : (pair + 1) * sources] = jnp.broadcast_to(
            total * scales[pair], (left.shape[0] - pixels, sources)
        )
    for half in range(2):
        for col in range(pixels // (2 * looks)):
            words = received[pl.ds(col * 2 + half, sources, stride=MESSAGE), :]
            for octet, value in enumerate((words >> 16, (words << 16) >> 16)):
                turned = aligned(value, half)
                for at in range(8):
                    pair = octet * 8 + at
                    row = (col * 2 + half) * looks
                    left[row : row + looks, pair * sources : (pair + 1) * sources] = (
                        turned[at * looks : (at + 1) * looks] * scales[pair]
                    )
    product = jnp.dot(
        left[...], right[...], precision=lax.Precision.HIGHEST, preferred_element_type=jnp.float32
    )
    out[...] = product[:pixels] * (1.0 / CODES)
    bias[...] = product[pixels:] * (1.0 / (CODES * band_pixels))


def invert(received, kept, swapped, pixels, band_pixels):
    total_pairs, dates = 2 * kept.shape[0], 2 * LANES
    vmem = pl.BlockSpec(memory_space=pltpu.VMEM)
    return pl.pallas_call(
        partial(invert_kernel, band_pixels),
        in_specs=[pl.BlockSpec(memory_space=pltpu.SMEM)] + [vmem] * 3,
        out_specs=[vmem] * 2,
        out_shape=[
            jax.ShapeDtypeStruct((pixels, dates), jnp.float32),
            jax.ShapeDtypeStruct((8, dates), jnp.float32),
        ],
        scratch_shapes=[
            pltpu.VMEM((pixels + 8, total_pairs), jnp.float32),
            pltpu.VMEM((total_pairs, dates), jnp.float32),
        ],
        compiler_params=pltpu.CompilerParams(vmem_limit_bytes=16 << 20),
        name="invert",
    )((lax.axis_index("date") % 2).reshape(1), received, kept, swapped)


def body(acquisitions, date_pairs, cycle_maps, inverse):
    group, _, height, width = acquisitions.shape
    devices = lax.axis_size("date")
    total_dates = group * devices
    pair_count, look_rows, look_cols = cycle_maps.shape
    rows = height // 2
    half = look_rows // 2

    def parts(images, start, stop):
        return images[:, :, :rows, start:stop], images[:, :, rows:, start:stop]

    def exchanged(pair):
        return passed_along(pair[0], "date", -1), passed_along(pair[1], "date", 1)

    low_pairs = passed_along(date_pairs, "date", 1)
    low_cycles = passed_along(cycle_maps, "date", 1)
    sent, left, low_pairs, low_cycles, date_pairs, inverse = lax.optimization_barrier(
        (parts(acquisitions, *CHUNKS[0]), acquisitions, low_pairs, low_cycles, date_pairs, inverse)
    )
    others = [exchanged(sent)]
    words, exponent = coded_inverse(inverse)
    line = exponent_line(exponent)
    for start, stop in CHUNKS[1:]:
        sent, left, words = lax.optimization_barrier((parts(left, start, stop), left, words))
        others.append(exchanged(sent))

    kept = sent_inverse(words)

    pairs = jnp.concatenate([date_pairs, low_pairs])
    gaps = (pairs[:, 1] - pairs[:, 0] + total_dates) % total_dates
    combos = pairs[:, 0] % group * group + gaps - 1
    late, words = lax.optimization_barrier((left, words))
    owned = [late[:, :, :, start:stop] for start, stop in CHUNKS]
    owned, combos = lax.optimization_barrier((owned, combos))
    looked = [(), ()]
    for (start, stop), own, received in zip(CHUNKS, owned, others):
        received, before = lax.optimization_barrier((received, looked[1]))
        upper = phases(start, stop, (0,), False, own, received[:1], looked[0])
        lower, upper = lax.optimization_barrier((received[1:], upper))
        rest = (upper, combos, cycle_maps, low_cycles, line) if stop == width else ()
        looked = [(upper,), (phases(start, stop, (1,), stop == width, own, lower, before, *rest),)]
    payload = looked[1][0]

    payload, kept = lax.optimization_barrier((payload, kept))
    swapped = lax.ppermute(kept, "date", [(at, at ^ 1) for at in range(devices)])
    received = lax.all_to_all(
        payload.reshape(devices, 1, -1), "date", split_axis=0, concat_axis=0, tiled=True
    ).reshape(payload.shape)
    out_cols = look_cols // devices
    row_count = lax.axis_size("row")
    result, bias = invert(received, kept, swapped, out_cols * look_rows, look_rows * look_cols * row_count)
    for step in range(1, row_count):
        result = result - passed_along(bias, "row", step)[:1]
    result = result - bias[:1]
    return result.reshape(out_cols, look_rows, total_dates)


def solution(mesh):
    return jax.shard_map(
        body,
        mesh=mesh,
        in_specs=(
            P("date", None, "row", None),
            P("date", None),
            P("date", "row", None),
            P(None, "date"),
        ),
        out_specs=P("date", "row", None),
        check_vma=False,
    )
```

```python
from functools import partial
import math

import jax
import jax.numpy as jnp
from jax import lax
from jax.experimental import pallas as pl
from jax.experimental.pallas import tpu as pltpu
from jax.sharding import PartitionSpec as P

LOOK_R = 4
LOOK_C = 16
TWO_PI = 2.0 * math.pi
CODES = 32767.0 / TWO_PI
CHUNKS = ((0, 1536), (1536, 2048))
STEP = 512
MESSAGE = 5
LANES = 128
ATAN = (
    0.9999993329,
    -0.3332985605,
    0.1994653599,
    -0.1390853351,
    0.0964200441,
    -0.0559098861,
    0.0218612288,
    -0.0040540580,
)


def passed_along(value, axis, steps):
    count = lax.axis_size(axis)
    pairs = [(source, (source + steps) % count) for source in range(count)]
    return lax.ppermute(value, axis, pairs)


def arctan2(y, x):
    wide, tall = jnp.abs(x), jnp.abs(y)
    larger = jnp.maximum(wide, tall)
    ratio = jnp.minimum(wide, tall) / jnp.where(larger == 0.0, 1.0, larger)
    square = ratio * ratio
    value = jnp.full_like(square, ATAN[-1])
    for factor in ATAN[-2::-1]:
        value = value * square + factor
    value = value * ratio
    value = jnp.where(tall > wide, 0.5 * math.pi - value, value)
    value = jnp.where(x < 0.0, math.pi - value, value)
    return jnp.where(y < 0.0, -value, value)


def phase_kernel(first_col, last, sides, final, own, *refs):
    refs = list(refs)
    others = [refs.pop(0) for _ in sides]
    earlier = [refs.pop(0) for _ in sides] if first_col else None
    if final:
        finished = refs.pop(0)
        combos, high_cycles, low_cycles, line, payload, held, arrived, images, high, low, picked = refs[:11]
        looked, cycles, sums, words = refs[11:]
    else:
        looked, held, arrived, images, high, low, picked = refs
    group, _, rows, _ = others[0].shape
    steps, width, _ = picked.shape
    looks = rows // LOOK_R
    pair_count = group * group
    step_cols = width // LOOK_C
    tiles = width // LANES
    copies = [
        pltpu.make_async_copy(
            other.at[:, :, :, pl.ds(step * width, width)],
            held.at[at * steps + step],
            arrived.at[at * steps + step],
        )
        for at, other in enumerate(others)
        for step in range(steps)
    ]
    for copy in copies:
        copy.start()
    shift = sides[0] if final else 0
    if final:
        looked[0] = finished[0]
    for step in range(steps):
        shape = picked.shape[1:]
        of = lax.broadcasted_iota(jnp.int32, shape, 0) // LOOK_C + first_col + step * step_cols
        chosen = of == lax.broadcasted_iota(jnp.int32, shape, 1)
        picked[step] = jnp.where(chosen, 1.0, 0.0).astype(jnp.bfloat16)

    def widen(source, start, row, col):
        @pl.loop(0, 2 * group)
        def _(index):
            date, part = index // 2, index % 2
            for tile in range(tiles):
                lanes = pl.ds(pl.multiple_of(col + tile * LANES, LANES), LANES)
                images[start + date, part, tile] = source[date, part, pl.ds(row, rows), lanes].astype(jnp.float32)

    @pl.loop(0, len(sides) * steps)
    def _(index):
        at, step_at = index // steps, index % steps
        half = at + sides[0]
        widen(own, half * group, pl.multiple_of(half * rows, rows), step_at * width)
        for piece, copy in enumerate(copies):
            pl.when(index == piece)(copy.wait)
        widen(held.at[index], (1 - half) * group, 0, 0)

        @pl.loop(0, tiles)
        def _(tile):
            lanes = pl.ds(pl.multiple_of(tile * LANES, LANES), LANES)
            for date in range(0, group, 2):
                totals = {}
                for block in range(looks // 8):
                    for step in range(LOOK_R):
                        lines = pl.ds(block * 8 * LOOK_R + step, 8, stride=LOOK_R)
                        seen = {
                            image: [images[image, part, tile, lines, :] for part in range(2)]
                            for image in range(date, date + group + 2)
                        }
                        for first in range(date, date + 2):
                            a0, a1 = seen[first]
                            for gap in range(group):
                                b0, b1 = seen[first + gap + 1]
                                re, im = a0 * b0 + a1 * b1, a1 * b0 - a0 * b1
                                for part, value in enumerate((re, im)):
                                    key = first, gap, part, block
                                    totals[key] = totals[key] + value if key in totals else value
                for first in range(date, date + 2):
                    for gap in range(group):
                        for part in range(2):
                            value = jnp.concatenate(
                                [totals[first, gap, part, block] for block in range(looks // 8)], axis=0
                            )
                            head = value.astype(jnp.bfloat16)
                            tail = (value - head.astype(jnp.float32)).astype(jnp.bfloat16)
                            start = (part * pair_count + first * group + gap) * looks
                            high[start : start + looks, lanes] = head
                            low[start : start + looks, lanes] = tail

        summed = jnp.dot(high[...], picked[step_at], preferred_element_type=jnp.float32)
        summed += jnp.dot(low[...], picked[step_at], preferred_element_type=jnp.float32)

        for place in range(len(sides)):

            @pl.when(index == place * steps)
            def _(place=place):
                looked[place + shift] = summed if earlier is None else earlier[place][0] + summed

        @pl.when(step_at > 0)
        def _():
            looked[at + shift] += summed

    if not final:
        return
    cycles[0] = TWO_PI * high_cycles[:, :looks, :].astype(jnp.float32).reshape(cycles.shape[1:])
    cycles[1] = TWO_PI * low_cycles[:, looks:, :].astype(jnp.float32).reshape(cycles.shape[1:])

    @pl.loop(0, 2)
    def _(half):
        taken = []
        for part in range(2):
            for pair in range(pair_count):
                start = (part * pair_count + combos[half * pair_count + pair]) * looks
                taken.append(looked[half, pl.ds(pl.multiple_of(start, 8), looks), :])
        real = jnp.concatenate(taken[:pair_count], axis=0)
        imag = jnp.concatenate(taken[pair_count:], axis=0)
        codes = jnp.round((arctan2(imag, real) - cycles[half] + math.pi) * CODES).T
        total = jnp.sum(codes, axis=0, keepdims=True).astype(jnp.int32)
        codes = codes.astype(jnp.int32)
        for octet in range(2):
            sums[pl.ds(2 * half + octet, 1), :] = total[:, octet * LANES : (octet + 1) * LANES]
        words[...] = (codes[:, :LANES] << 16) | (codes[:, LANES:] & 0xFFFF)
        count = last // 2
        for col in range(2):
            payload[pl.ds(2 * col + half, count, stride=MESSAGE), :] = words[pl.ds(col, count, stride=2), :]

    total = sums[...]
    for step in (8, 4, 2, 1):
        total += pltpu.roll(total, LANES - step, 1)
    lane = lax.broadcasted_iota(jnp.int32, (1, LANES), 1) % looks
    full = line[0:1, :]
    for row in range(4):
        moved = pltpu.roll(total, row, 1)[row : row + 1]
        full = jnp.where(lane == row, moved, full)
    payload[pl.ds(4, last // 2, stride=MESSAGE), :] = jnp.broadcast_to(full, (last // 2, LANES))


def phases(start, stop, sides, final, own, others, earlier, *rest):
    group, _, height, _ = own.shape
    rows = height // 2
    looked_cols = LANES
    looks = rows // LOOK_R
    tiles = STEP // LANES
    pair_count = group * group
    steps = (stop - start) // STEP
    vmem = pl.BlockSpec(memory_space=pltpu.VMEM)
    in_specs = [vmem] + [pl.BlockSpec(memory_space=pl.ANY)] * len(others) + [vmem] * len(earlier)
    looked_shape = (len(sides), 2 * pair_count * looks, looked_cols)
    out_shape = jax.ShapeDtypeStruct(looked_shape, jnp.float32)
    scratch = [
        pltpu.VMEM((len(sides) * steps, group, 2, rows, STEP), jnp.bfloat16),
        pltpu.SemaphoreType.DMA((len(sides) * steps,)),
        pltpu.VMEM((2 * group, 2, tiles, rows, LANES), jnp.float32),
        pltpu.VMEM((2 * pair_count * looks, STEP), jnp.bfloat16),
        pltpu.VMEM((2 * pair_count * looks, STEP), jnp.bfloat16),
        pltpu.VMEM((steps, STEP, looked_cols), jnp.bfloat16),
    ]
    if final:
        in_specs += [vmem, pl.BlockSpec(memory_space=pltpu.SMEM)] + [vmem] * 3
        out_shape = jax.ShapeDtypeStruct((looked_cols // 2 * MESSAGE, LANES), jnp.int32)
        scratch += [
            pltpu.VMEM((2, 2 * pair_count * looks, looked_cols), jnp.float32),
            pltpu.VMEM((2, pair_count * looks, looked_cols), jnp.float32),
            pltpu.VMEM((8, LANES), jnp.int32),
            pltpu.VMEM((looked_cols, LANES), jnp.int32),
        ]
    return pl.pallas_call(
        partial(phase_kernel, start // LOOK_C, stop // LOOK_C, sides, final),
        in_specs=in_specs,
        out_specs=vmem,
        out_shape=out_shape,
        scratch_shapes=scratch,
        compiler_params=pltpu.CompilerParams(vmem_limit_bytes=16 << 20),
        cost_estimate=pl.CostEstimate(
            flops=8 * pair_count * rows * len(sides) * (stop - start),
            bytes_accessed=group * 4 * height * (stop - start) * 2,
            transcendentals=0,
        ),
        name="phases",
    )(own, *others, *earlier, *rest)


def coded_inverse(inverse):
    turned = inverse.T
    peak = jnp.max(jnp.abs(turned), axis=1, keepdims=True)
    exponent = jnp.clip(jnp.floor(jnp.log2(peak)) + 1.0, -100.0, 100.0)
    codes = jnp.round(turned * jnp.exp2(-exponent) * 32767.0).astype(jnp.int32)
    words = (codes[:, :LANES] << 16) | (codes[:, LANES:] & 0xFFFF)
    return words, exponent[:, 0].astype(jnp.int32)


def exponent_line(exponent):
    spread = exponent.reshape(2, -1).T
    spread = jnp.pad(spread, ((0, 0), (4, LANES // spread.shape[0] - 6)))
    return jnp.broadcast_to(spread.reshape(1, LANES), (8, LANES))


def sent_inverse(words):
    devices = lax.axis_size("date")
    per = words.shape[0] // 2
    sent = jnp.broadcast_to(words.reshape(1, 2, per, LANES), (devices // 2, 2, per, LANES))
    got = lax.all_to_all(
        sent.reshape(devices, per, LANES), "date", split_axis=0, concat_axis=0, tiled=True
    ).reshape(-1, LANES)
    return got


def invert_kernel(band_pixels, side, received, kept, swapped, out, bias, left, right):
    pair_count = 16
    per = pair_count // 2
    sources = kept.shape[0] // per
    looks = LANES * 2 // pair_count
    pixels = out.shape[0]

    def aligned(words, half):
        value = words.astype(jnp.float32)
        return (pltpu.roll(value, sources - 1, 0) if half else value).T

    for at in range(per):
        for owner, source in ((side[0], kept), (1 - side[0], swapped)):
            words = source[pl.ds(at, sources, stride=per), :]
            place = pl.ds(pl.multiple_of((owner * per + at) * sources, 8), sources)
            right[place, :LANES] = (words >> 16).astype(jnp.float32)
            right[place, LANES:] = ((words << 16) >> 16).astype(jnp.float32)
    line = received[pl.ds(4, sources, stride=MESSAGE), :]
    lines = aligned(line, 0), aligned(line, 1)
    scales = []
    for pair in range(pair_count):
        octet, at = pair // 8, pair % 8 * looks
        scales.append(jnp.exp2(lines[0][at + 4 + octet : at + 5 + octet]) * (1.0 / 32767.0))
        total = lines[0][at + octet : at + octet + 1] + lines[1][at + 2 + octet : at + 3 + octet]
        left[pixels:, pair * sources : (pair + 1) * sources] = jnp.broadcast_to(
            total * scales[pair], (left.shape[0] - pixels, sources)
        )
    for half in range(2):
        for col in range(pixels // (2 * looks)):
            words = received[pl.ds(col * 2 + half, sources, stride=MESSAGE), :]
            for octet, value in enumerate((words >> 16, (words << 16) >> 16)):
                turned = aligned(value, half)
                for at in range(8):
                    pair = octet * 8 + at
                    row = (col * 2 + half) * looks
                    left[row : row + looks, pair * sources : (pair + 1) * sources] = (
                        turned[at * looks : (at + 1) * looks] * scales[pair]
                    )
    product = jnp.dot(
        left[...], right[...], precision=lax.Precision.HIGHEST, preferred_element_type=jnp.float32
    )
    out[...] = product[:pixels] * (1.0 / CODES)
    bias[...] = product[pixels:] * (1.0 / (CODES * band_pixels))


def invert(received, kept, swapped, pixels, band_pixels):
    total_pairs, dates = 2 * kept.shape[0], 2 * LANES
    vmem = pl.BlockSpec(memory_space=pltpu.VMEM)
    return pl.pallas_call(
        partial(invert_kernel, band_pixels),
        in_specs=[pl.BlockSpec(memory_space=pltpu.SMEM)] + [vmem] * 3,
        out_specs=[vmem] * 2,
        out_shape=[
            jax.ShapeDtypeStruct((pixels, dates), jnp.float32),
            jax.ShapeDtypeStruct((8, dates), jnp.float32),
        ],
        scratch_shapes=[
            pltpu.VMEM((pixels + 8, total_pairs), jnp.float32),
            pltpu.VMEM((total_pairs, dates), jnp.float32),
        ],
        compiler_params=pltpu.CompilerParams(vmem_limit_bytes=16 << 20),
        name="invert",
    )((lax.axis_index("date") % 2).reshape(1), received, kept, swapped)


def body(acquisitions, date_pairs, cycle_maps, inverse):
    group, _, height, width = acquisitions.shape
    devices = lax.axis_size("date")
    total_dates = group * devices
    pair_count, look_rows, look_cols = cycle_maps.shape
    rows = height // 2
    half = look_rows // 2

    def parts(images, start, stop):
        return images[:, :, :rows, start:stop], images[:, :, rows:, start:stop]

    def exchanged(pair):
        return passed_along(pair[0], "date", -1), passed_along(pair[1], "date", 1)

    low_pairs = passed_along(date_pairs, "date", 1)
    low_cycles = passed_along(cycle_maps, "date", 1)
    sent, left, low_pairs, low_cycles, date_pairs, inverse = lax.optimization_barrier(
        (parts(acquisitions, *CHUNKS[0]), acquisitions, low_pairs, low_cycles, date_pairs, inverse)
    )
    others = [exchanged(sent)]
    words, exponent = coded_inverse(inverse)
    line = exponent_line(exponent)
    for start, stop in CHUNKS[1:]:
        sent, left, words = lax.optimization_barrier((parts(left, start, stop), left, words))
        others.append(exchanged(sent))

    kept = sent_inverse(words)

    pairs = jnp.concatenate([date_pairs, low_pairs])
    gaps = (pairs[:, 1] - pairs[:, 0] + total_dates) % total_dates
    combos = pairs[:, 0] % group * group + gaps - 1
    late, words = lax.optimization_barrier((left, words))
    owned = [late[:, :, :, start:stop] for start, stop in CHUNKS]
    owned, combos = lax.optimization_barrier((owned, combos))
    looked = [(), ()]
    for (start, stop), own, received in zip(CHUNKS, owned, others):
        first, before = received[:1], looked[1]
        if before:
            first, before = lax.optimization_barrier((first, before))
        upper = phases(start, stop, (0,), False, own, first, looked[0])
        lower, upper = lax.optimization_barrier((received[1:], upper))
        rest = (upper, combos, cycle_maps, low_cycles, line) if stop == width else ()
        looked = [(upper,), (phases(start, stop, (1,), stop == width, own, lower, before, *rest),)]
    payload = looked[1][0]

    payload, kept = lax.optimization_barrier((payload, kept))
    swapped = lax.ppermute(kept, "date", [(at, at ^ 1) for at in range(devices)])
    received = lax.all_to_all(
        payload.reshape(devices, 1, -1), "date", split_axis=0, concat_axis=0, tiled=True
    ).reshape(payload.shape)
    out_cols = look_cols // devices
    row_count = lax.axis_size("row")
    result, bias = invert(received, kept, swapped, out_cols * look_rows, look_rows * look_cols * row_count)
    for step in range(1, row_count):
        result = result - passed_along(bias, "row", step)[:1]
    result = result - bias[:1]
    return result.reshape(out_cols, look_rows, total_dates)


def solution(mesh):
    return jax.shard_map(
        body,
        mesh=mesh,
        in_specs=(
            P("date", None, "row", None),
            P("date", None),
            P("date", "row", None),
            P(None, "date"),
        ),
        out_specs=P("date", "row", None),
        check_vma=False,
    )
```
